512 devices in a mesh: dp: 8 (over y, core), seq: 16 (over z), tensor: 4 (over x).
Axes of the slice: x: 4, y: 4, z: 16, core: 2. Of those that a mesh axis runs over, the one named last changes fastest.
Arguments:
- queries: bfloat16 [8, 2048, 8192], P('dp', 'seq', 'tensor'), may hold values from -6 to 6
- keys: bfloat16 [8, 2048, 1024], P('dp', 'seq', 'tensor'), may hold values from -6 to 6
- output_gradient: bfloat16 [8, 2048, 8192], P('dp', 'seq', 'tensor'), may hold values from -6 to 6
- normed: bfloat16 [8, 2048, 4096], P('dp', 'seq', 'tensor'), may hold values from -6 to 6
- document_length: int32 [8, 8], P('dp'), may hold values from 1 to 1536, 2048 in all within a row
- codes: bfloat16 [4096, 1024], P(None, 'tensor'), may hold values from -8 to 7, as said below
- scales: float32 [32, 1024], P(None, 'tensor'), may hold values from 0.0015 to 0.006
- adapter_down: bfloat16 [4096, 64], P('tensor'), may hold values from -0.09375 to 0.09375
- adapter_up: bfloat16 [64, 1024], P(None, 'tensor'), may hold values from -0.75 to 0.75
Outputs:
- d_normed: bfloat16 [8, 2048, 4096], P('dp', 'seq', 'tensor')
- grad_a: float32 [4096, 64], P('tensor')
- grad_b: float32 [64, 1024], P(None, 'tensor')
The draws below stay inside these ranges and needn't reach their ends.
Inputs may be any that keep to these rules, and one draw needn't show every extreme that they name: `codes`: whole-numbered levels.
All inputs are finite; a program needn't handle non-finite values.
Results may differ from the reference program's by a relative error of at most 0.02.
Values may be sent and summed in bfloat16 or wider, within the bound.
A program may use at most 64 MiB of HBM per device.

```python
import math
import jax
import jax.numpy as jnp
import numpy as np
from jax import lax

MODEL_WIDTH = 4096
HQ = 64
VALUE_HEADS = 8
HEAD_SIZE = 128
ADAPTER_RANK = 64
GROUP_SIZE = 128
NDOC = 8
ROWS = 8
LENGTH = 2048


def draw_queries(key, part):
    key = jax.random.fold_in(key, 11)
    result = jnp.clip(jax.random.normal(key, (ROWS, LENGTH, HQ * HEAD_SIZE), jnp.float32), -6.0, 6.0)
    return result.astype(jnp.bfloat16)


def draw_keys(key, part):
    key = jax.random.fold_in(key, 12)
    result = jnp.clip(jax.random.normal(key, (ROWS, LENGTH, VALUE_HEADS * HEAD_SIZE), jnp.float32), -6.0, 6.0)
    return result.astype(jnp.bfloat16)


def draw_codes(key, part):
    key = jax.random.fold_in(key, 13)
    levels = jax.random.randint(key, (MODEL_WIDTH, VALUE_HEADS * HEAD_SIZE), -8, 8, jnp.int32)
    return levels.astype(jnp.float32).astype(jnp.bfloat16)


def shard_levels(key, extent, pieces, smallest, top_value):
    loudness = 1.0
    for axis_at, shards_of in pieces:
        draws = jax.random.uniform(jax.random.fold_in(jax.random.fold_in(key, 6), axis_at), (shards_of,), jnp.float32, smallest / len(pieces), top_value / len(pieces))
        loudness = loudness * jnp.repeat(jnp.exp(draws), extent[axis_at] // shards_of).reshape((-1,) + (1,) * (len(extent) - 1 - axis_at))
    return loudness


def length_profile(number_of, total, reach, lean):
    loads = [(1 << 20) // math.isqrt(rank ** lean) + 1 for rank in range(2, number_of + 1)]
    surplus, given = total - reach - (number_of - 1), [1] * (number_of - 1)
    while surplus > 0:
        movable = [i for i in range(number_of - 1) if given[i] < reach]
        whole, left = sum([loads[i] for i in movable]), surplus
        for i in movable:
            more = min(reach - given[i], max(1, left * loads[i] // whole), surplus)
            given[i] = given[i] + more
            surplus = surplus - more
    return np.array([reach] + given)


def ragged(rng, number_of, total, most, skew):
    if number_of == 2:
        one = jax.random.randint(rng, (), max(1, total - most), min(most, total - 1) + 1)
        return jnp.stack([one, total - one])
    lengths = jnp.asarray(length_profile(number_of, total, most, skew), jnp.int32)
    pairs = (number_of - 1) // 2
    donor, receiver = lengths[1:1 + 2 * pairs:2], lengths[2:2 + 2 * pairs:2]
    room = jnp.minimum(donor - 1, most - receiver)
    passed = jax.random.randint(jax.random.fold_in(rng, 1), (pairs,), 0, 1 << 20) % (room + 1)
    lengths = lengths.at[1:1 + 2 * pairs:2].set(donor - passed).at[2:2 + 2 * pairs:2].set(receiver + passed)
    return lengths[jax.random.permutation(jax.random.fold_in(rng, 2), number_of)]


def scatter_about(own_key, dims, width, limit, cuts=(), held_as=jnp.bfloat16):
    factor_of = shard_levels(own_key, dims, cuts, -0.22, 0.18) if cuts else 1.0
    values = jax.random.normal(own_key, dims, jnp.float32) * width * factor_of
    return jnp.minimum(jnp.maximum(values, -limit), limit).astype(held_as)


def setup_inputs(seed: int = 0) -> dict:
    streams_of = jax.random.split(jax.random.key(seed), 10)
    queries = draw_queries(jax.random.fold_in(streams_of[9], 71), 0)
    keys = draw_keys(jax.random.fold_in(streams_of[9], 71), 0)
    output_gradient = scatter_about(streams_of[2], (ROWS, LENGTH, HQ * HEAD_SIZE), 1.0, 6.0, ((0, 8), (1, 16), (2, 4)))
    normed = scatter_about(streams_of[3], (ROWS, LENGTH, MODEL_WIDTH), 1.0, 6.0, ((0, 8), (1, 16), (2, 4)))
    document_length = jax.vmap(lambda own: ragged(own, NDOC, LENGTH, 3 * LENGTH // 4, 2))(jax.random.split(streams_of[4], ROWS)).reshape((ROWS, NDOC)).astype(jnp.int32)
    codes = draw_codes(jax.random.fold_in(streams_of[9], 71), 0)
    scales = jnp.clip(jnp.exp(math.log(0.006) - 1.3862944 * jax.random.uniform(streams_of[6], (MODEL_WIDTH // GROUP_SIZE, VALUE_HEADS * HEAD_SIZE), jnp.float32) ** shard_levels(streams_of[6], (MODEL_WIDTH // GROUP_SIZE, VALUE_HEADS * HEAD_SIZE), ((1, 4),), -0.2, 0.2)), 0.0015, 0.006)
    adapter_down = scatter_about(streams_of[7], (MODEL_WIDTH, ADAPTER_RANK), MODEL_WIDTH ** -0.5, 0.09375, ((0, 4),))
    adapter_up = scatter_about(streams_of[8], (ADAPTER_RANK, VALUE_HEADS * HEAD_SIZE), ADAPTER_RANK ** -0.5, 0.75, ((1, 4),))
    return {"queries": queries, "keys": keys, "output_gradient": output_gradient, "normed": normed, "document_length": document_length, "codes": codes, "scales": scales, "adapter_down": adapter_down, "adapter_up": adapter_up}


NEG = -1e+30

def segment_ids(document_length, length):
    bounds = jnp.cumsum(document_length)
    positions = jnp.arange(length, dtype=jnp.int32)
    return lax.optimization_barrier(jnp.sum((positions[:, None] >= bounds[None, :]).astype(jnp.int32), axis=1))

def head_values(query, key_rows, grad_rows, seg, block):
    length = key_rows.shape[0]
    positions = jnp.arange(length, dtype=jnp.int32)
    inverse = 1.0 / math.sqrt(query.shape[1])

    def step(total, index):
        first = index * block
        rows = lax.dynamic_slice_in_dim(query, first, block, 0)
        grads = lax.dynamic_slice_in_dim(grad_rows, first, block, 0)
        row_seg = lax.dynamic_slice_in_dim(seg, first, block, 0)
        row_pos = lax.dynamic_slice_in_dim(positions, first, block, 0)
        allowed = (row_seg[:, None] == seg[None, :]) & (positions[None, :] <= row_pos[:, None])
        scores = jnp.dot(rows, key_rows.T, preferred_element_type=jnp.float32) * inverse
        scores = jnp.where(allowed, scores, NEG)
        peak = lax.optimization_barrier(jnp.max(scores, axis=1, keepdims=True))
        weights = jnp.where(allowed, jnp.exp(scores - peak), 0.0)
        probs = (weights / lax.optimization_barrier(jnp.sum(weights, axis=1, keepdims=True))).astype(jnp.bfloat16)
        return (total + jnp.dot(probs.T, grads, preferred_element_type=jnp.float32), None)
    start = jnp.zeros((length, grad_rows.shape[1]), jnp.float32)
    total, unused = lax.scan(step, start, jnp.arange(length // block, dtype=jnp.int32))
    return total

def row_values(query, key_rows, grad_rows, lens):
    seg = segment_ids(lens, LENGTH)
    block = math.gcd(LENGTH, 512)
    group = HQ // VALUE_HEADS
    query_h = query.reshape(LENGTH, HQ, HEAD_SIZE)
    key_h = key_rows.reshape(LENGTH, VALUE_HEADS, HEAD_SIZE)
    grad_h = grad_rows.reshape(LENGTH, HQ, HEAD_SIZE)

    def one_head(head):
        return head_values(query_h[:, head], key_h[:, head // group], grad_h[:, head], seg, block)
    each = lax.map(one_head, jnp.arange(HQ, dtype=jnp.int32))
    summed = lax.optimization_barrier(jnp.sum(each.reshape(VALUE_HEADS, group, LENGTH, HEAD_SIZE), axis=1))
    return jnp.transpose(summed, (1, 0, 2)).reshape(LENGTH, VALUE_HEADS * HEAD_SIZE).astype(jnp.bfloat16)

def reference(queries, keys, output_gradient, normed, document_length, codes, scales, adapter_down, adapter_up):
    values = lax.map(lambda items: row_values(items[0], items[1], items[2], items[3]), (queries, keys, output_gradient, document_length))
    value_gradient = values.reshape(ROWS * LENGTH, VALUE_HEADS * HEAD_SIZE)
    flat_rows = normed.reshape(ROWS * LENGTH, MODEL_WIDTH)
    weight = (codes.astype(jnp.float32).reshape(MODEL_WIDTH // GROUP_SIZE, GROUP_SIZE, VALUE_HEADS * HEAD_SIZE) * scales[:, None, :]).reshape(MODEL_WIDTH, VALUE_HEADS * HEAD_SIZE).astype(jnp.bfloat16)
    lowrank_input = jnp.dot(flat_rows, adapter_down, preferred_element_type=jnp.float32).astype(jnp.bfloat16)
    projection_gradient = jnp.dot(value_gradient, adapter_up.T, preferred_element_type=jnp.float32).astype(jnp.bfloat16)
    base = jnp.dot(value_gradient, weight.T, preferred_element_type=jnp.float32)
    adapter_branch = 2.0 * jnp.dot(projection_gradient, adapter_down.T, preferred_element_type=jnp.float32)
    d_normed = (base + adapter_branch).astype(jnp.bfloat16).reshape(ROWS, LENGTH, MODEL_WIDTH)
    factor = 2.0 / math.sqrt(ROWS * LENGTH)
    grad_a = jnp.dot(flat_rows.T, projection_gradient, preferred_element_type=jnp.float32) * factor
    grad_b = jnp.dot(lowrank_input.T, value_gradient, preferred_element_type=jnp.float32) * factor
    return (d_normed, grad_a, grad_b)
```

```python
import functools
import math

import jax
import jax.numpy as jnp
from jax import lax
from jax.experimental import pallas as pl
from jax.experimental.pallas import tpu as pltpu
from jax.sharding import PartitionSpec as P

MESH = pl.DeviceIdType.MESH
HEAD = 128
GROUP = 128
KV = 2
NEG = -1e30
F32 = jnp.float32
BF16 = jnp.bfloat16
NT = (((1,), (1,)), ((), ()))
TN = (((0,), (0,)), ((), ()))


def dot(a, b):
    return jnp.dot(a, b, preferred_element_type=F32)


def dot_general(a, b, dims):
    return lax.dot_general(a, b, dims, preferred_element_type=F32)


def kernel(
    shape,
    q_hbm, k_hbm, g_hbm, n_hbm, len_ref, codes_hbm, scales_hbm, down_hbm, up_hbm,
    dn_ref, ga_ref, gb_ref,
    kbuf, qv, qt, gv, nv, codes, scales, down, up, wst, wfull, bias_ref,
    m_ref, l_ref, ms_ref, w_ref, rs_l, rs_r, xa_buf, gx_buf, dv_buf,
    a_src, a_rcv, b_src, b_rcv, c_buf, d_buf,
    local_sem, f_send, f_recv, bk_send, bk_recv, ls, lr, rs, rr,
    w_send, w_recv, wc_send, wc_recv, xa_send, xa_recv, gx_send, gx_recv,
    dv_send, dv_recv, a_send, a_recv, b_send, b_recv, c_send, c_recv, d_send, d_recv,
):
    D, S, T = shape
    half = S // 2
    B = kbuf.shape[2]
    pairs = qt.shape[0]
    per_kv = pairs // KV
    feats = nv.shape[1]
    rank = up.shape[0]
    cols = up.shape[1]
    hf = feats // 2
    dp = lax.axis_index("dp")
    seq = lax.axis_index("seq")
    ten = lax.axis_index("tensor")
    core = lax.rem(dp, 2)
    sibling = dp + 1 - 2 * core
    right = {"seq": lax.rem(seq + 1, S)}
    left = {"seq": lax.rem(seq + S - 1, S)}

    def remote(src, dst, send, recv, where):
        return pltpu.make_async_remote_copy(
            src_ref=src, dst_ref=dst, send_sem=send, recv_sem=recv,
            device_id=where, device_id_type=MESH,
        )

    def local(src, dst, i):
        return pltpu.make_async_copy(src, dst, local_sem.at[i])

    in_k = [local(k_hbm.at[:, pl.ds(g * HEAD, HEAD)], kbuf.at[0, g], g) for g in range(KV)]
    in_q = local(q_hbm, qv, 2)
    in_codes = local(codes_hbm, codes, 3)
    in_scales = local(scales_hbm, scales, 4)
    in_n = local(n_hbm, nv, 5)
    in_down = local(down_hbm, down, 6)
    in_up = local(up_hbm, up, 7)
    in_g = [
        local(
            g_hbm.at[:, pl.ds(h * HEAD, HEAD)],
            gv.at[h // 2, pl.ds((h % 2) * B, B), :],
            8 + h,
        )
        for h in range(2 * pairs)
    ]
    for c in in_k + [in_q, in_codes, in_scales, in_n, in_down, in_up] + in_g:
        c.start()

    barrier = pltpu.get_barrier_semaphore()

    def greet(axis, me, size):
        def one(k, carry):
            pl.semaphore_signal(
                barrier, inc=1, device_id={axis: lax.rem(me + k, size)}, device_id_type=MESH
            )
            return carry
        lax.fori_loop(1, size, one, 0)

    greet("seq", seq, S)
    greet("tensor", ten, T)
    greet("dp", dp, D)
    for c in in_k:
        c.wait()
    pl.semaphore_wait(barrier, S + T + D - 3)

    def fwd(t, g):
        return remote(kbuf.at[t, g], kbuf.at[t + 1, g], f_send.at[t, g], f_recv.at[t + 1, g], right)

    def bwd(t, g):
        a = S - t if isinstance(t, int) and t == 0 else S - t
        src = kbuf.at[lax.rem(a, S), g]
        return remote(src, kbuf.at[S - 1 - t, g], bk_send.at[t, g], bk_recv.at[t + 1, g], left)

    fwd(0, 0).start()
    bwd(0, 1).start()
    fwd(0, 1).start()
    bwd(0, 0).start()

    ipos = seq * B + lax.broadcasted_iota(jnp.int32, (1, B), 1)
    start = jnp.zeros((1, B), jnp.int32)
    bound = jnp.int32(0)
    for d in range(len_ref.shape[1] - 1):
        bound = bound + len_ref[0, d]
        start = jnp.where(ipos >= bound, bound, start)
    jrow = lax.broadcasted_iota(jnp.int32, (B, B), 0)
    scale = math.log2(math.e) / math.sqrt(HEAD)

    in_q.wait()
    for h in range(2 * pairs):
        qt[h // 2, :, (h % 2) * B : (h % 2 + 1) * B] = qv[:, h * HEAD : (h + 1) * HEAD].T
    m_ref[...] = jnp.full(m_ref.shape, NEG, F32)
    l_ref[...] = jnp.zeros(l_ref.shape, F32)

    def attend(slots, t):
        for n, slot in enumerate(slots):
            jpos = lax.rem(seq - slot + S, S) * B + jrow
            allowed = (jpos >= start) & (jpos <= ipos)
            bias_ref[n] = jnp.where(allowed, 0.0, NEG).astype(F32)

        def pair(hp, carry):
            g = lax.div(hp, per_kv)
            wide = qt[hp]
            ts = []
            for n, slot in enumerate(slots):
                b = bias_ref[n]
                ts.append(dot(kbuf[slot, g], wide) * scale + jnp.concatenate([b, b], axis=1))
            peak = ts[0] if len(ts) == 1 else jnp.maximum(ts[0], ts[1])
            old = m_ref[hp]
            new = jnp.maximum(old, jnp.max(peak, axis=0, keepdims=True))
            total = l_ref[hp] * jnp.exp2(old - new)
            ws = [jnp.exp2(x - new) for x in ts]
            both = ws[0] if len(ws) == 1 else ws[0] + ws[1]
            l_ref[hp] = total + jnp.sum(both, axis=0, keepdims=True)
            for w, slot in zip(ws, slots):
                w_ref[slot, hp] = w.astype(BF16)
            m_ref[hp] = new
            ms_ref[t, hp] = new
            return carry

        lax.fori_loop(0, pairs, pair, 0)

    attend([0], 0)

    in_n.wait()
    in_down.wait()
    xa_buf[0] = dot_general(down[...], nv[...], NT).astype(BF16)

    def xa_copy(k):
        return remote(
            xa_buf.at[0], xa_buf.at[k], xa_send.at[k], xa_recv.at[k], {"tensor": lax.rem(ten + k, T)}
        )

    for k in range(1, T):
        xa_copy(k).start()

    in_codes.wait()
    in_scales.wait()

    def dequantised(first, n, put):
        def one(i, carry):
            row = pl.multiple_of(first + i * GROUP, GROUP)
            block = codes[pl.ds(row, GROUP), :].astype(F32)
            put(i, (block * scales[pl.ds(lax.div(row, GROUP), 1), :]).astype(BF16))
            return carry
        lax.fori_loop(0, n // GROUP, one, 0)

    def w_copy(k):
        return remote(
            wst.at[k], wfull.at[k, core], w_send.at[k], w_recv.at[k], {"tensor": lax.rem(ten + k, T)}
        )

    def wc_copy(k, h):
        return remote(wfull.at[k, h], wfull.at[k, h], wc_send.at[k], wc_recv.at[k], {"dp": sibling})

    for k in range(1, T):
        def put(i, value, k=k):
            wst[k, pl.ds(pl.multiple_of(i * GROUP, GROUP), GROUP), :] = value
        dequantised(lax.rem(ten + k, T) * feats + core * hf, hf, put)
        w_copy(k).start()
    for h in range(2):
        def put(i, value, h=h):
            wfull[0, h, pl.ds(pl.multiple_of(i * GROUP, GROUP), GROUP), :] = value
        dequantised(ten * feats + h * hf, hf, put)

    def pass_on(t, f1, b0):
        fwd(t - 1, 0).wait_recv()
        fwd(t, 0).start()
        bwd(t - 1, 1).wait_recv()
        bwd(t, 1).start()
        fwd(t - 1, 1).wait_recv()
        if f1:
            fwd(t, 1).start()
        bwd(t - 1, 0).wait_recv()
        if b0:
            bwd(t, 0).start()

    def ring(t, carry):
        pass_on(t, True, True)
        attend([t, S - t], t)
        return carry

    lax.fori_loop(1, half - 1, ring, 0)
    pass_on(half - 1, False, False)
    attend([half - 1, half + 1], half - 1)
    fwd(half - 1, 0).wait_recv()
    bwd(half - 1, 1).wait_recv()
    attend([half], half)

    l_ref[...] = 1.0 / l_ref[...]
    for c in in_g:
        c.wait()

    def partial(slot, t, g):
        total = None
        for i in range(per_kv):
            hp = g * per_kv + i
            factor = jnp.exp2(ms_ref[t, hp] - m_ref[hp]) * l_ref[hp]
            p = (w_ref[slot, hp].astype(F32) * factor).astype(BF16)
            one = dot(p, gv[hp])
            total = one if total is None else total + one
        return total

    def go_l(u, g):
        return remote(rs_l.at[u, g], rs_l.at[u + 1, g], ls.at[u, g], lr.at[u + 1, g], left)

    def go_r(u, g):
        return remote(rs_r.at[u, g], rs_r.at[u + 1, g], rs.at[u, g], rr.at[u + 1, g], right)

    rs_l[0, 0] = partial(half, half, 0).astype(BF16)
    go_l(0, 0).start()
    rs_r[0, 1] = partial(half, half, 1).astype(BF16)
    go_r(0, 1).start()

    def reduce_step(u, first):
        a, b, t = half - u, half + u, half - u
        al = [partial(a, t, g) for g in range(KV)]
        br = [partial(b, t, g) for g in range(KV)]
        go_l(u - 1, 0).wait_recv()
        rs_l[u, 0] = (al[0] + rs_l[u, 0].astype(F32)).astype(BF16)
        go_l(u, 0).start()
        go_r(u - 1, 1).wait_recv()
        rs_r[u, 1] = (br[1] + rs_r[u, 1].astype(F32)).astype(BF16)
        go_r(u, 1).start()
        if first:
            rs_l[u, 1] = al[1].astype(BF16)
        else:
            go_l(u - 1, 1).wait_recv()
            rs_l[u, 1] = (al[1] + rs_l[u, 1].astype(F32)).astype(BF16)
        go_l(u, 1).start()
        if first:
            rs_r[u, 0] = br[0].astype(BF16)
        else:
            go_r(u - 1, 0).wait_recv()
            rs_r[u, 0] = (br[0] + rs_r[u, 0].astype(F32)).astype(BF16)
        go_r(u, 0).start()

    reduce_step(1, True)

    def reduce_loop(u, carry):
        reduce_step(u, False)
        return carry

    lax.fori_loop(2, half, reduce_loop, 0)

    own = [partial(0, 0, g) for g in range(KV)]
    for k in range(1, T):
        xa_copy(k).wait_recv()
    xat = xa_buf[0].astype(F32)
    for k in range(1, T):
        xat = xat + xa_buf[k].astype(F32)
    xat = xat.astype(BF16)
    for k in range(1, T):
        w_copy(k).wait_recv()
        wc_copy(k, core).start()
    in_up.wait()
    for g in range(KV):
        go_l(half - 1, g).wait_recv()
        go_r(half - 1, g).wait_recv()
        dv_buf[0, :, g * HEAD : (g + 1) * HEAD] = (
            own[g] + rs_l[half, g].astype(F32) + rs_r[half, g].astype(F32)
        ).astype(BF16)

    dv = dv_buf[0]
    gx_buf[0] = dot_general(up[...], dv, NT).astype(BF16)

    def gx_copy(k):
        return remote(
            gx_buf.at[0], gx_buf.at[k], gx_send.at[k], gx_recv.at[k], {"tensor": lax.rem(ten + k, T)}
        )

    def dv_copy(k):
        return remote(
            dv_buf.at[0], dv_buf.at[k], dv_send.at[k], dv_recv.at[k], {"tensor": lax.rem(ten + k, T)}
        )

    for k in range(1, T):
        gx_copy(k).start()
    for k in range(1, T):
        dv_copy(k).start()
    per = a_src.shape[1]
    across = (feats + cols) // 128

    def tile_at(i, j):
        n = i * across + j
        return n // per, n % per

    part_b = dot(xat, dv)
    for i in range(rank // 16):
        for j in range(cols // 128):
            p, q = tile_at(i, feats // 128 + j)
            a_src[p, q] = part_b[i * 16 : i * 16 + 16, j * 128 : j * 128 + 128].astype(BF16)
    for k in range(1, T):
        gx_copy(k).wait_recv()
    gpt = gx_buf[0].astype(F32)
    for k in range(1, T):
        gpt = gpt + gx_buf[k].astype(F32)
    gpt = gpt.astype(BF16)
    for j in range(feats // 128):
        part_a = dot(gpt, nv[:, j * 128 : j * 128 + 128])
        for i in range(rank // 16):
            p, q = tile_at(i, j)
            a_src[p, q] = part_a[i * 16 : i * 16 + 16].astype(BF16)

    def a_copy(k):
        peer = lax.rem(dp + k, D)
        return remote(a_src.at[peer], a_rcv.at[k], a_send.at[k], a_recv.at[k], {"dp": peer})

    for k in range(1, D):
        a_copy(k).start()
    for k in range(1, D):
        a_copy(k).wait_recv()
    total = a_src[dp].astype(F32)
    for k in range(1, D):
        total = total + a_rcv[k].astype(F32)
    b_src[...] = total.astype(BF16)

    owners = [j * S // per for j in range(per)]

    def b_copy(j):
        away = lax.rem(owners[j] - seq + S, S)
        return remote(
            b_src.at[j], b_rcv.at[away], b_send.at[j], b_recv.at[away], {"seq": jnp.int32(owners[j])}
        )

    mine = jnp.int32(0)
    owner = seq == owners[0]
    for j in range(1, per):
        mine = jnp.where(seq == owners[j], j, mine)
        owner = owner | (seq == owners[j])

    for j in range(per):
        @pl.when(seq != owners[j])
        def _():
            b_copy(j).start()

    def c_copy(k):
        return remote(
            c_buf.at[mine], c_buf.at[mine], c_send.at[k], c_recv.at[mine], {"seq": lax.rem(seq + k, S)}
        )

    @pl.when(owner)
    def _():
        total = b_src[mine].astype(F32)
        for k in range(1, S):
            remote(
                b_src.at[0], b_rcv.at[k], b_send.at[0], b_recv.at[k], {"seq": lax.rem(seq + k, S)}
            ).wait_recv()
            total = total + b_rcv[k].astype(F32)
        c_buf[mine] = total.astype(BF16)
        for k in range(1, S):
            c_copy(k).start()

    for j in range(per):
        @pl.when(seq != owners[j])
        def _():
            remote(
                b_src.at[j], c_buf.at[j], c_send.at[0], c_recv.at[j], {"seq": jnp.int32(owners[j])}
            ).wait_recv()

    def d_copy(k):
        return remote(
            c_buf, d_buf.at[dp], d_send.at[k], d_recv.at[dp], {"dp": lax.rem(dp + k, D)}
        )

    for k in range(1, D):
        d_copy(k).start()
    d_buf[dp] = c_buf[...]

    gp = gpt.T
    for k in range(1, T):
        dv_copy(k).wait_recv()
        wc_copy(k, 1 - core).wait_recv()
    width = min(256, hf)
    for n in range(feats // width):
        h, row = n * width // hf, n * width % hf
        at = slice(n * width, (n + 1) * width)
        total = 2.0 * dot(gp, down[:, at])
        for k in range(T):
            total = total + dot_general(dv_buf[k], wfull[k, h, row : row + width, :], NT)
        dn_ref[:, at] = total.astype(BF16)

    for k in range(1, D):
        peer = lax.rem(dp + k, D)
        remote(c_buf, d_buf.at[peer], d_send.at[k], d_recv.at[peer], {"dp": peer}).wait_recv()
    factor = 2.0 / math.sqrt(D * S * B)
    for i in range(rank // 16):
        for j in range(across):
            p, q = tile_at(i, j)
            value = d_buf[p, q].astype(F32) * factor
            if j < feats // 128:
                ga_ref[i * 16 : i * 16 + 16, j * 128 : j * 128 + 128] = value
            else:
                c = j * 128 - feats
                gb_ref[i * 16 : i * 16 + 16, c : c + 128] = value

    for t in range(half):
        fwd(t, 0).wait_send()
        bwd(t, 1).wait_send()
        go_l(t, 0).wait_send()
        go_r(t, 1).wait_send()
        if t < half - 1:
            fwd(t, 1).wait_send()
            bwd(t, 0).wait_send()
        if t > 0:
            go_l(t, 1).wait_send()
            go_r(t, 0).wait_send()
    for k in range(1, T):
        xa_copy(k).wait_send()
        w_copy(k).wait_send()
        wc_copy(k, core).wait_send()
        gx_copy(k).wait_send()
        dv_copy(k).wait_send()
    for k in range(1, D):
        a_copy(k).wait_send()
        d_copy(k).wait_send()
    for j in range(per):
        @pl.when(seq != owners[j])
        def _():
            b_copy(j).wait_send()

    @pl.when(owner)
    def _():
        for k in range(1, S):
            c_copy(k).wait_send()


def body(
    shape, queries, keys, output_gradient, normed, document_length, codes, scales,
    adapter_down, adapter_up,
):
    D, S, T = shape
    B = queries.shape[1]
    heads = queries.shape[2] // HEAD
    pairs = heads // 2
    feats = normed.shape[2]
    rank, cols = adapter_up.shape
    half = S // 2
    per = (rank // 16) * ((feats + cols) // 128) // D
    anyspace = pl.BlockSpec(memory_space=pl.ANY)
    vmem = pl.BlockSpec(memory_space=pltpu.VMEM)
    smem = pl.BlockSpec(memory_space=pltpu.SMEM)
    dma = pltpu.SemaphoreType.DMA
    d_normed, grad_a, grad_b = pl.pallas_call(
        functools.partial(kernel, shape),
        out_shape=(
            jax.ShapeDtypeStruct((B, feats), BF16),
            jax.ShapeDtypeStruct((rank, feats), F32),
            jax.ShapeDtypeStruct((rank, cols), F32),
        ),
        in_specs=[anyspace] * 4 + [smem] + [anyspace] * 4,
        out_specs=(vmem, vmem, vmem),
        scratch_shapes=[
            pltpu.VMEM((S, KV, B, HEAD), BF16),
            pltpu.VMEM((B, heads * HEAD), BF16),
            pltpu.VMEM((pairs, HEAD, 2 * B), BF16),
            pltpu.VMEM((pairs, 2 * B, HEAD), BF16),
            pltpu.VMEM((B, feats), BF16),
            pltpu.VMEM(codes.shape, BF16),
            pltpu.VMEM(scales.shape, F32),
            pltpu.VMEM((rank, feats), BF16),
            pltpu.VMEM((rank, cols), BF16),
            pltpu.VMEM((T, feats // 2, cols), BF16),
            pltpu.VMEM((T, 2, feats // 2, cols), BF16),
            pltpu.VMEM((2, B, B), F32),
            pltpu.VMEM((pairs, 1, 2 * B), F32),
            pltpu.VMEM((pairs, 1, 2 * B), F32),
            pltpu.VMEM((half + 1, pairs, 1, 2 * B), F32),
            pltpu.VMEM((S, pairs, B, 2 * B), BF16),
            pltpu.VMEM((half + 1, KV, B, HEAD), BF16),
            pltpu.VMEM((half + 1, KV, B, HEAD), BF16),
            pltpu.VMEM((T, rank, B), BF16),
            pltpu.VMEM((T, rank, B), BF16),
            pltpu.VMEM((T, B, cols), BF16),
            pltpu.VMEM((D, per, 16, 128), BF16),
            pltpu.VMEM((D, per, 16, 128), BF16),
            pltpu.VMEM((per, 16, 128), BF16),
            pltpu.VMEM((S, 16, 128), BF16),
            pltpu.VMEM((per, 16, 128), BF16),
            pltpu.VMEM((D, per, 16, 128), BF16),
            dma((8 + heads,)),
            dma((half + 1, KV)),
            dma((half + 1, KV)),
            dma((half + 1, KV)),
            dma((half + 1, KV)),
            dma((half + 1, KV)),
            dma((half + 1, KV)),
            dma((half + 1, KV)),
            dma((half + 1, KV)),
            dma((T,)),
            dma((T,)),
            dma((T,)),
            dma((T,)),
            dma((T,)),
            dma((T,)),
            dma((T,)),
            dma((T,)),
            dma((T,)),
            dma((T,)),
            dma((D,)),
            dma((D,)),
            dma((per,)),
            dma((S,)),
            dma((S,)),
            dma((per,)),
            dma((D,)),
            dma((D,)),
        ],
        compiler_params=pltpu.CompilerParams(
            collective_id=0, has_side_effects=True, vmem_limit_bytes=40 * 1024 * 1024
        ),
        name="value_backward",
    )(
        queries[0], keys[0], output_gradient[0], normed[0], document_length, codes, scales,
        adapter_down.T, adapter_up,
    )
    return d_normed[None], grad_a.T, grad_b


def solution(mesh):
    shape = tuple(mesh.shape[a] for a in ("dp", "seq", "tensor"))
    split = P("dp", "seq", "tensor")
    placed = (
        split, split, split, split,
        P("dp", None), P(None, "tensor"), P(None, "tensor"), P("tensor", None), P(None, "tensor"),
    )
    return jax.shard_map(
        functools.partial(body, shape),
        mesh=mesh,
        in_specs=placed,
        out_specs=(split, P("tensor", None), P(None, "tensor")),
        check_vma=False,
    )
```

```python
import functools
import math

import jax
import jax.numpy as jnp
from jax import lax
from jax.experimental import pallas as pl
from jax.experimental.pallas import tpu as pltpu
from jax.sharding import PartitionSpec as P

MESH = pl.DeviceIdType.MESH
HEAD = 128
GROUP = 128
KV = 2
NEG = -1e30
F32 = jnp.float32
BF16 = jnp.bfloat16
NT = (((1,), (1,)), ((), ()))
TN = (((0,), (0,)), ((), ()))


def dot(a, b):
    return jnp.dot(a, b, preferred_element_type=F32)


def dot_general(a, b, dims):
    return lax.dot_general(a, b, dims, preferred_element_type=F32)


class Tree:
    def __init__(self, size):
        half, last = size // 2, size - 1
        if size == 16:
            self.parent = {3: 0, 1: 0, 6: 3, 2: 3, 8: 6, 4: 6, 7: 6, 5: 6}
            self.after = {3: [1], 6: [2]}
            self.far_relays = {3: [15], 6: [12]}
            self.final = [7, 5, 8, 4]
            self.far_planes = [15, 12]
            self.far_leaves = [14, 13, 11, 10, 9]
        else:
            self.parent = {2: 0, 1: 2}
            self.after = {2: []}
            self.far_relays = {2: [last]}
            self.final = [1]
            self.far_planes = [last]
            self.far_leaves = []
        self.relays = list(self.after)
        self.children = {a: [b for b in self.parent if self.parent[b] == a] for a in range(half + 1)}
        self.least = {b: min(self.below(b)) for b in self.parent}
        self.wrapped = list(range(half - 1))
        self.last = last
        self.half = half
        self.far_index = {}
        for a in range(size):
            edges = [(b, c) for c in self.wrapped for (x, b) in self.far_edges(c) if x == a]
            for e, (b, c) in enumerate(edges):
                self.far_index[a, b, c] = e
        self.far_most = max(self.far_index.values()) + 1

    def below(self, b):
        return [b] + [x for child in self.children[b] for x in self.below(child)]

    def far_parent(self, plane, c):
        if plane - c <= self.half:
            return None
        if plane == self.last:
            return c
        if plane in (14, 12) or (plane, c) == (13, 4):
            return 15
        return 12

    def far_edges(self, c):
        return [(self.far_parent(b, c), b) for b in range(c + self.half + 1, self.last + 1)]

    def far_children(self, plane, c):
        return [b for a, b in self.far_edges(c) if a == plane]


def kernel(
    shape,
    q_hbm, k_hbm, g_hbm, n_hbm, len_hbm, codes_hbm, scales_hbm, down_hbm, up_hbm,
    dn_ref, ga_ref, gb_ref,
    len_ref, kbuf, qv, qt, gv, nv, codes, scales, down, up, wst, wfull, bias_ref,
    m_ref, l_ref, ms_ref, w_ref, acc_ref, rs_out, rs_in, rs_far, xa_buf, gx_buf, dv_buf,
    a_src, a_rcv, b_src, b_rcv, c_buf, d_buf,
    local_sem, k_send, k_recv, s_send, s_recv, far_recv,
    w_send, w_recv, wc_send, wc_recv, xa_send, xa_recv, gx_send, gx_recv,
    dv_send, dv_recv, a_send, a_recv, b_send, b_recv, c_send, c_recv, d_send, d_recv,
):
    D, S, T = shape
    half = S // 2
    tree = Tree(S)
    B = kbuf.shape[2]
    pairs = qt.shape[0]
    per_kv = pairs // KV
    feats = nv.shape[1]
    rank = up.shape[0]
    cols = up.shape[1]
    hf = feats // 2
    dp = lax.axis_index("dp")
    seq = lax.axis_index("seq")
    ten = lax.axis_index("tensor")
    core = lax.rem(dp, 2)
    sibling = dp + 1 - 2 * core
    near = min(3, half)
    last = S - 1

    def remote(src, dst, send, recv, where):
        return pltpu.make_async_remote_copy(
            src_ref=src, dst_ref=dst, send_sem=send, recv_sem=recv,
            device_id=where, device_id_type=MESH,
        )

    def local(src, dst, i):
        return pltpu.make_async_copy(src, dst, local_sem.at[i])

    in_k = [local(k_hbm.at[:, pl.ds(g * HEAD, HEAD)], kbuf.at[0, g], g) for g in range(KV)]
    in_q = local(q_hbm, qv, 2)
    in_codes = local(codes_hbm, codes, 3)
    in_scales = local(scales_hbm, scales, 4)
    in_n = local(n_hbm, nv, 5)
    in_down = local(down_hbm, down, 6)
    in_up = local(up_hbm, up, 7)
    in_len = local(len_hbm, len_ref, 8)
    in_g = [
        local(
            g_hbm.at[:, pl.ds(h * HEAD, HEAD)],
            gv.at[h // 2, pl.ds((h % 2) * B, B), :],
            9 + h,
        )
        for h in range(2 * pairs)
    ]
    due = {"k": in_k, "q": [in_q, in_len], "n": [in_n, in_down], "w": [in_codes, in_scales]}
    due.update({"g": in_g, "up": [in_up]})
    for group in ("k", "q", "n", "w", "g", "up"):
        for c in due[group]:
            c.start()

    def ready(group):
        for c in due.pop(group):
            c.wait()

    sent = []
    coming = {}

    def send(copies, group=None):
        for c in copies:
            c.start()
        sent.extend(copies)
        if group:
            coming[group] = copies

    def arrive(group):
        for c in coming.pop(group):
            c.wait_recv()

    barrier = pltpu.get_barrier_semaphore()

    def greet(axis, me, size):
        def one(k, carry):
            pl.semaphore_signal(
                barrier, inc=1, device_id={axis: lax.rem(me + k, size)}, device_id_type=MESH
            )
            return carry
        lax.fori_loop(1, size, one, 0)

    for k in range(1, near + 1):
        for away in (k, S - k):
            pl.semaphore_signal(
                barrier, inc=1, device_id={"seq": lax.rem(seq + away, S)}, device_id_type=MESH
            )
    greet("tensor", ten, T)
    greet("dp", dp, D)
    remotes = [c for c in tree.wrapped if near <= c < last - near]
    if remotes:
        @pl.when(seq == last)
        def _():
            for c in remotes:
                pl.semaphore_signal(
                    barrier, inc=1, device_id={"seq": jnp.int32(c)}, device_id_type=MESH
                )

    def k_copy(a, b, where):
        return remote(kbuf.at[a], kbuf.at[b], k_send.at[b], k_recv.at[b], {"seq": where})

    def runs(b):
        return lax.rem(seq - b + S, S) + tree.least[b] <= last

    def pass_down(a):
        for b in tree.children[a]:
            @pl.when(lax.rem(seq - a + S, S) + tree.least[b] <= last)
            def _(b=b):
                k_copy(a, b, lax.rem(seq + b - a + S, S)).start()

    def k_arrive(b):
        k_copy(0, b, seq).wait_recv()

    def far_copy(c, a, b):
        here, there = a - c, b - c
        return remote(
            kbuf.at[here], kbuf.at[there], k_send.at[S + tree.far_index[a, b, c]], k_recv.at[there],
            {"seq": jnp.int32(b)},
        )

    def pass_far(a):
        for c in tree.wrapped:
            if tree.far_parent(a, c) is None:
                continue
            k_arrive(a - c)
            for b in tree.far_children(a, c):
                far_copy(c, a, b).start()

    ready("q")
    ready("k")
    ipos = seq * B + lax.broadcasted_iota(jnp.int32, (1, B), 1)
    start = jnp.zeros((1, B), jnp.int32)
    bound = jnp.int32(0)
    for d in range(len_ref.shape[1] - 1):
        bound = bound + len_ref[0, d]
        start = jnp.where(ipos >= bound, bound, start)
    jrow = lax.broadcasted_iota(jnp.int32, (B, B), 0)
    scale = math.log2(math.e) / math.sqrt(HEAD)

    for h in range(2 * pairs):
        qt[h // 2, :, (h % 2) * B : (h % 2 + 1) * B] = qv[:, h * HEAD : (h + 1) * HEAD].T
    m_ref[...] = jnp.full(m_ref.shape, NEG, F32)
    l_ref[...] = jnp.zeros(l_ref.shape, F32)

    def attend(slot):
        jpos = lax.rem(seq - slot + S, S) * B + jrow
        allowed = (jpos >= start) & (jpos <= ipos)
        bias = jnp.where(allowed, 0.0, NEG).astype(F32)
        bias_ref[...] = jnp.concatenate([bias, bias], axis=1)

        def pair(hp, carry):
            g = lax.div(hp, per_kv)
            x = dot(kbuf[slot, g], qt[hp]) * scale + bias_ref[...]
            old = m_ref[hp]
            new = jnp.maximum(old, jnp.max(x, axis=0, keepdims=True))
            w = jnp.exp2(x - new)
            l_ref[hp] = l_ref[hp] * jnp.exp2(old - new) + jnp.sum(w, axis=0, keepdims=True)
            w_ref[slot, hp] = w.astype(BF16)
            m_ref[hp] = new
            ms_ref[slot, hp] = new
            return carry

        lax.fori_loop(0, pairs, pair, 0)

    def attend_on_arrival(slot):
        @pl.when(seq >= slot)
        def _():
            k_arrive(slot)
            attend(slot)

    attend(0)
    greeted = 2 * near + T + D - 2
    if remotes:
        greeted = greeted + ((seq >= remotes[0]) & (seq <= remotes[-1])).astype(jnp.int32)
    pl.semaphore_wait(barrier, greeted)
    pass_down(0)
    for c in tree.wrapped:
        @pl.when(seq == c)
        def _(c=c):
            far_copy(c, c, last).start()

    ready("n")
    xa_buf[0] = dot_general(down[...], nv[...], NT).astype(BF16)

    def xa_copy(k):
        return remote(
            xa_buf.at[0], xa_buf.at[k], xa_send.at[k], xa_recv.at[k], {"tensor": lax.rem(ten + k, T)}
        )

    send([xa_copy(k) for k in range(1, T)], "xa")

    ready("w")

    def dequantised(first, n, put):
        def one(i, carry):
            row = pl.multiple_of(first + i * GROUP, GROUP)
            block = codes[pl.ds(row, GROUP), :].astype(F32)
            put(i, (block * scales[pl.ds(lax.div(row, GROUP), 1), :]).astype(BF16))
            return carry
        lax.fori_loop(0, n // GROUP, one, 0)

    def w_copy(k):
        return remote(
            wst.at[k], wfull.at[k, core], w_send.at[k], w_recv.at[k], {"tensor": lax.rem(ten + k, T)}
        )

    def wc_copy(k, h):
        return remote(wfull.at[k, h], wfull.at[k, h], wc_send.at[k], wc_recv.at[k], {"dp": sibling})

    for k in range(1, T):
        def put(i, value, k=k):
            wst[k, pl.ds(pl.multiple_of(i * GROUP, GROUP), GROUP), :] = value
        dequantised(lax.rem(ten + k, T) * feats + core * hf, hf, put)
        send([w_copy(k)])
    coming["w"] = [w_copy(k) for k in range(1, T)]
    for h in range(2):
        def put(i, value, h=h):
            wfull[0, h, pl.ds(pl.multiple_of(i * GROUP, GROUP), GROUP), :] = value
        dequantised(ten * feats + h * hf, hf, put)

    for a in tree.relays:
        @pl.when(runs(a))
        def _(a=a):
            k_arrive(a)
            pass_down(a)
            @pl.when(seq >= a)
            def _():
                attend(a)
        for b in tree.after[a]:
            attend_on_arrival(b)
        for plane in tree.far_relays[a]:
            @pl.when(seq == plane)
            def _(plane=plane):
                pass_far(plane)
    relay = seq < 0
    for plane in tree.far_planes:
        relay = relay | (seq == plane)

    def far_slot(i, carry):
        slot = last - i

        @pl.when(seq >= slot)
        def _():
            @pl.when(jnp.logical_not(relay & (seq - slot <= tree.wrapped[-1])))
            def _():
                k_arrive(slot)
            attend(slot)
        return carry

    lax.fori_loop(0, last - half, far_slot, 0)
    for b in tree.final:
        attend_on_arrival(b)

    l_ref[...] = 1.0 / l_ref[...]
    ready("g")

    def partial(slot):
        for g in range(KV):
            total = None
            for i in range(per_kv):
                hp = g * per_kv + i
                factor = jnp.exp2(ms_ref[slot, hp] - m_ref[hp]) * l_ref[hp]
                p = (w_ref[slot, hp].astype(F32) * factor).astype(BF16)
                one = dot(p, gv[hp])
                total = one if total is None else total + one
            acc_ref[g] = total

    def s_copy(a, b, where):
        return remote(rs_out.at[b], rs_in.at[b], s_send.at[b], s_recv.at[b], {"seq": where})

    def up_to(a, b):
        return s_copy(a, b, lax.rem(seq + a - b + S, S))

    def gather(a, keep):
        if a == 0:
            partial(0)
        else:
            @pl.when(seq >= a)
            def _():
                partial(a)

            @pl.when(seq < a)
            def _():
                acc_ref[...] = jnp.zeros(acc_ref.shape, F32)
        for b in tree.children[a]:
            @pl.when(lax.rem(seq - a + S, S) + tree.least[b] <= last)
            def _(b=b):
                s_copy(a, b, seq).wait_recv()
                acc_ref[...] += rs_in[b].astype(F32)
        if keep:
            rs_out[a] = acc_ref[...].astype(BF16)

    def far_up(c, a, b):
        slot, e = b - c, tree.far_index[a, b, c]
        return remote(
            rs_out.at[slot], rs_far.at[e], s_send.at[slot], far_recv.at[e], {"seq": jnp.int32(a)}
        )

    def send_up(b):
        @pl.when(runs(b))
        def _():
            gather(b, True)
            up_to(tree.parent[b], b).start()

    def far_leaf(c, a, b):
        partial(b - c)
        rs_out[b - c] = acc_ref[...].astype(BF16)
        far_up(c, a, b).start()

    def far_gather(a, c):
        partial(a - c)
        for b in tree.far_children(a, c):
            far_up(c, a, b).wait_recv()
            acc_ref[...] += rs_far[tree.far_index[a, b, c]].astype(F32)
        rs_out[a - c] = acc_ref[...].astype(BF16)
        far_up(c, tree.far_parent(a, c), a).start()

    for b in reversed(tree.final):
        send_up(b)
    for plane in tree.far_leaves:
        @pl.when(seq == plane)
        def _(plane=plane):
            for c in reversed(tree.wrapped):
                a = tree.far_parent(plane, c)
                if a is not None:
                    far_leaf(c, a, plane)
    for a in reversed(tree.relays):
        for plane in tree.far_relays[a]:
            @pl.when(seq == plane)
            def _(plane=plane):
                for c in reversed(tree.wrapped):
                    if tree.far_parent(plane, c) is not None:
                        far_gather(plane, c)
        for b in tree.after[a]:
            send_up(b)
        send_up(a)

    arrive("xa")
    xat = xa_buf[0].astype(F32)
    for k in range(1, T):
        xat = xat + xa_buf[k].astype(F32)
    xat = xat.astype(BF16)
    arrive("w")
    send([wc_copy(k, core) for k in range(1, T)])
    coming["wc"] = [wc_copy(k, 1 - core) for k in range(1, T)]
    ready("up")
    gather(0, False)
    for c in tree.wrapped:
        @pl.when(seq == c)
        def _(c=c):
            far_up(c, c, last).wait_recv()
            acc_ref[...] += rs_far[tree.far_index[c, last, c]].astype(F32)
    for g in range(KV):
        dv_buf[0, :, g * HEAD : (g + 1) * HEAD] = acc_ref[g].astype(BF16)

    dv = dv_buf[0]
    gx_buf[0] = dot_general(up[...], dv, NT).astype(BF16)

    def gx_copy(k):
        return remote(
            gx_buf.at[0], gx_buf.at[k], gx_send.at[k], gx_recv.at[k], {"tensor": lax.rem(ten + k, T)}
        )

    def dv_copy(k):
        return remote(
            dv_buf.at[0], dv_buf.at[k], dv_send.at[k], dv_recv.at[k], {"tensor": lax.rem(ten + k, T)}
        )

    send([gx_copy(k) for k in range(1, T)], "gx")
    send([dv_copy(k) for k in range(1, T)], "dv")
    per = a_src.shape[1]
    across = (feats + cols) // 128

    def tile_at(i, j):
        n = i * across + j
        return n // per, n % per

    part_b = dot(xat, dv)
    for i in range(rank // 16):
        for j in range(cols // 128):
            p, q = tile_at(i, feats // 128 + j)
            a_src[p, q] = part_b[i * 16 : i * 16 + 16, j * 128 : j * 128 + 128].astype(BF16)
    arrive("gx")
    gpt = gx_buf[0].astype(F32)
    for k in range(1, T):
        gpt = gpt + gx_buf[k].astype(F32)
    gpt = gpt.astype(BF16)
    for j in range(feats // 128):
        part_a = dot(gpt, nv[:, j * 128 : j * 128 + 128])
        for i in range(rank // 16):
            p, q = tile_at(i, j)
            a_src[p, q] = part_a[i * 16 : i * 16 + 16].astype(BF16)

    def a_copy(k):
        peer = lax.rem(dp + k, D)
        return remote(a_src.at[peer], a_rcv.at[k], a_send.at[k], a_recv.at[k], {"dp": peer})

    send([a_copy(k) for k in range(1, D)], "a")
    arrive("a")
    total = a_src[dp].astype(F32)
    for k in range(1, D):
        total = total + a_rcv[k].astype(F32)
    b_src[...] = total.astype(BF16)

    owners = [j * S // per for j in range(per)]

    def b_copy(j):
        away = lax.rem(owners[j] - seq + S, S)
        return remote(
            b_src.at[j], b_rcv.at[away], b_send.at[j], b_recv.at[away], {"seq": jnp.int32(owners[j])}
        )

    mine = jnp.int32(0)
    owner = seq == owners[0]
    for j in range(1, per):
        mine = jnp.where(seq == owners[j], j, mine)
        owner = owner | (seq == owners[j])

    for j in range(per):
        @pl.when(seq != owners[j])
        def _():
            b_copy(j).start()

    def c_copy(k):
        return remote(
            c_buf.at[mine], c_buf.at[mine], c_send.at[k], c_recv.at[mine], {"seq": lax.rem(seq + k, S)}
        )

    @pl.when(owner)
    def _():
        total = b_src[mine].astype(F32)
        for k in range(1, S):
            remote(
                b_src.at[0], b_rcv.at[k], b_send.at[0], b_recv.at[k], {"seq": lax.rem(seq + k, S)}
            ).wait_recv()
            total = total + b_rcv[k].astype(F32)
        c_buf[mine] = total.astype(BF16)
        for k in range(1, S):
            c_copy(k).start()

    for j in range(per):
        @pl.when(seq != owners[j])
        def _():
            remote(
                b_src.at[j], c_buf.at[j], c_send.at[0], c_recv.at[j], {"seq": jnp.int32(owners[j])}
            ).wait_recv()

    def d_copy(k):
        return remote(
            c_buf, d_buf.at[dp], d_send.at[k], d_recv.at[dp], {"dp": lax.rem(dp + k, D)}
        )

    send([d_copy(k) for k in range(1, D)])

    def d_from(k):
        peer = lax.rem(dp + k, D)
        return remote(c_buf, d_buf.at[peer], d_send.at[k], d_recv.at[peer], {"dp": peer})

    coming["d"] = [d_from(k) for k in range(1, D)]
    d_buf[dp] = c_buf[...]

    gp = gpt.T
    arrive("dv")
    arrive("wc")
    width = min(256, hf)
    for n in range(feats // width):
        h, row = n * width // hf, n * width % hf
        at = slice(n * width, (n + 1) * width)
        total = 2.0 * dot(gp, down[:, at])
        for k in range(T):
            total = total + dot_general(dv_buf[k], wfull[k, h, row : row + width, :], NT)
        dn_ref[:, at] = total.astype(BF16)

    arrive("d")
    factor = 2.0 / math.sqrt(D * S * B)
    for i in range(rank // 16):
        for j in range(across):
            p, q = tile_at(i, j)
            value = d_buf[p, q].astype(F32) * factor
            if j < feats // 128:
                ga_ref[i * 16 : i * 16 + 16, j * 128 : j * 128 + 128] = value
            else:
                c = j * 128 - feats
                gb_ref[i * 16 : i * 16 + 16, c : c + 128] = value

    for c in sent:
        c.wait_send()
    for b in range(1, half + 1):
        a = tree.parent[b]

        @pl.when(lax.rem(seq - a + S, S) + tree.least[b] <= last)
        def _(a=a, b=b):
            k_copy(a, b, seq).wait_send()

        @pl.when(runs(b))
        def _(b=b):
            up_to(a, b).wait_send()
    for c in tree.wrapped:
        for a, b in tree.far_edges(c):
            @pl.when(seq == a)
            def _(a=a, b=b, c=c):
                far_copy(c, a, b).wait_send()

            @pl.when(seq == b)
            def _(a=a, b=b, c=c):
                far_up(c, a, b).wait_send()
    for j in range(per):
        @pl.when(seq != owners[j])
        def _():
            b_copy(j).wait_send()

    @pl.when(owner)
    def _():
        for k in range(1, S):
            c_copy(k).wait_send()


def body(
    shape, queries, keys, output_gradient, normed, document_length, codes, scales,
    adapter_down, adapter_up,
):
    D, S, T = shape
    B = queries.shape[1]
    heads = queries.shape[2] // HEAD
    pairs = heads // 2
    feats = normed.shape[2]
    rank, cols = adapter_up.shape
    half = S // 2
    far = Tree(S).far_most
    per = (rank // 16) * ((feats + cols) // 128) // D
    hbm = pl.BlockSpec(memory_space=pltpu.HBM)
    vmem = pl.BlockSpec(memory_space=pltpu.VMEM)
    dma = pltpu.SemaphoreType.DMA
    d_normed, grad_a, grad_b = pl.pallas_call(
        functools.partial(kernel, shape),
        out_shape=(
            jax.ShapeDtypeStruct((B, feats), BF16),
            jax.ShapeDtypeStruct((rank, feats), F32),
            jax.ShapeDtypeStruct((rank, cols), F32),
        ),
        in_specs=[hbm] * 9,
        out_specs=(vmem, vmem, vmem),
        scratch_shapes=[
            pltpu.SMEM(document_length.shape, jnp.int32),
            pltpu.VMEM((S, KV, B, HEAD), BF16),
            pltpu.VMEM((B, heads * HEAD), BF16),
            pltpu.VMEM((pairs, HEAD, 2 * B), BF16),
            pltpu.VMEM((pairs, 2 * B, HEAD), BF16),
            pltpu.VMEM((B, feats), BF16),
            pltpu.VMEM(codes.shape, BF16),
            pltpu.VMEM(scales.shape, F32),
            pltpu.VMEM((rank, feats), BF16),
            pltpu.VMEM((rank, cols), BF16),
            pltpu.VMEM((T, feats // 2, cols), BF16),
            pltpu.VMEM((T, 2, feats // 2, cols), BF16),
            pltpu.VMEM((B, 2 * B), F32),
            pltpu.VMEM((pairs, 1, 2 * B), F32),
            pltpu.VMEM((pairs, 1, 2 * B), F32),
            pltpu.VMEM((S, pairs, 1, 2 * B), F32),
            pltpu.VMEM((S, pairs, B, 2 * B), BF16),
            pltpu.VMEM((KV, B, HEAD), F32),
            pltpu.VMEM((S, KV, B, HEAD), BF16),
            pltpu.VMEM((half + 1, KV, B, HEAD), BF16),
            pltpu.VMEM((far, KV, B, HEAD), BF16),
            pltpu.VMEM((T, rank, B), BF16),
            pltpu.VMEM((T, rank, B), BF16),
            pltpu.VMEM((T, B, cols), BF16),
            pltpu.VMEM((D, per, 16, 128), BF16),
            pltpu.VMEM((D, per, 16, 128), BF16),
            pltpu.VMEM((per, 16, 128), BF16),
            pltpu.VMEM((S, 16, 128), BF16),
            pltpu.VMEM((per, 16, 128), BF16),
            pltpu.VMEM((D, per, 16, 128), BF16),
            dma((9 + heads,)),
            dma((S + far,)),
            dma((S,)),
            dma((S,)),
            dma((half + 1,)),
            dma((far,)),
            dma((T,)),
            dma((T,)),
            dma((T,)),
            dma((T,)),
            dma((T,)),
            dma((T,)),
            dma((T,)),
            dma((T,)),
            dma((T,)),
            dma((T,)),
            dma((D,)),
            dma((D,)),
            dma((per,)),
            dma((S,)),
            dma((S,)),
            dma((per,)),
            dma((D,)),
            dma((D,)),
        ],
        compiler_params=pltpu.CompilerParams(
            collective_id=0, has_side_effects=True, vmem_limit_bytes=40 * 1024 * 1024
        ),
        name="value_backward",
    )(
        *(
            pltpu.with_memory_space_constraint(x, pltpu.HBM)
            for x in (
                queries[0], keys[0], output_gradient[0], normed[0], document_length, codes,
                scales, adapter_down.T, adapter_up,
            )
        )
    )
    return d_normed[None], grad_a.T, grad_b


def solution(mesh):
    shape = tuple(mesh.shape[a] for a in ("dp", "seq", "tensor"))
    split = P("dp", "seq", "tensor")
    placed = (
        split, split, split, split,
        P("dp", None), P(None, "tensor"), P(None, "tensor"), P("tensor", None), P(None, "tensor"),
    )
    return jax.shard_map(
        functools.partial(body, shape),
        mesh=mesh,
        in_specs=placed,
        out_specs=(split, P("tensor", None), P(None, "tensor")),
        check_vma=False,
    )
```

```python
import functools
import math

import jax
import jax.numpy as jnp
from jax import lax
from jax.experimental import pallas as pl
from jax.experimental.pallas import tpu as pltpu
from jax.sharding import PartitionSpec as P

MESH = pl.DeviceIdType.MESH
HEAD = 128
GROUP = 128
KV = 2
NEG = -1e30
F32 = jnp.float32
BF16 = jnp.bfloat16
NT = (((1,), (1,)), ((), ()))
TN = (((0,), (0,)), ((), ()))


def dot(a, b):
    return jnp.dot(a, b, preferred_element_type=F32)


def dot_general(a, b, dims):
    return lax.dot_general(a, b, dims, preferred_element_type=F32)


class Tree:
    def __init__(self, size):
        if size == 16:
            self.parent = {3: 0, 1: 0, 11: 0, 6: 3, 2: 3, 12: 11, 10: 11, 9: 11, 8: 6, 4: 6, 7: 6, 5: 6}
            self.after = {3: [], 11: [3, 1, 11], 6: [2, 6]}
            self.final = [12, 10, 9, 7, 5, 8, 4]
            self.near = [1, 2, 3]
            self.up = [8, 4, 7, 5, 12, 10, 9, 2, 1, 6, 11, 3]
            self.far = 11
        else:
            self.parent = {2: 0, 1: 2, 3: 0}
            self.after = {2: [2]}
            self.final = [1, 3]
            self.near = [1, 2]
            self.up = [1, 3, 2]
            self.far = None
        self.relays = list(self.after)
        self.children = {a: [b for b in self.parent if self.parent[b] == a] for a in range(size)}
        self.least = {b: min(self.below(b)) for b in self.parent}

    def below(self, b):
        return [b] + [x for child in self.children[b] for x in self.below(child)]


def kernel(
    shape,
    q_hbm, k_hbm, g_hbm, n_hbm, len_hbm, codes_hbm, scales_hbm, down_hbm, up_hbm,
    dn_ref, ga_ref, gb_ref,
    len_ref, kbuf, qv, qt, gv, nv, codes, scales, down, up, wst, wfull, bias_ref,
    m_ref, l_ref, ms_ref, w_ref, acc_ref, rs_out, rs_in, xa_buf, gx_buf, dv_buf,
    a_src, a_rcv, b_src, b_rcv, c_buf, d_buf,
    local_sem, k_send, k_recv, s_send, s_recv,
    w_send, w_recv, wc_send, wc_recv, xa_send, xa_recv, gx_send, gx_recv,
    dv_send, dv_recv, a_send, a_recv, b_send, b_recv, c_send, c_recv, d_send, d_recv,
):
    D, S, T = shape
    tree = Tree(S)
    B = kbuf.shape[2]
    pairs = qt.shape[0]
    per_kv = pairs // KV
    feats = nv.shape[1]
    rank = up.shape[0]
    cols = up.shape[1]
    hf = feats // 2
    dp = lax.axis_index("dp")
    seq = lax.axis_index("seq")
    ten = lax.axis_index("tensor")
    core = lax.rem(dp, 2)
    sibling = dp + 1 - 2 * core
    last = S - 1

    def remote(src, dst, send, recv, where):
        return pltpu.make_async_remote_copy(
            src_ref=src, dst_ref=dst, send_sem=send, recv_sem=recv,
            device_id=where, device_id_type=MESH,
        )

    def local(src, dst, i):
        return pltpu.make_async_copy(src, dst, local_sem.at[i])

    in_k = [local(k_hbm.at[:, pl.ds(g * HEAD, HEAD)], kbuf.at[0, g], g) for g in range(KV)]
    in_q = local(q_hbm, qv, 2)
    in_codes = local(codes_hbm, codes, 3)
    in_scales = local(scales_hbm, scales, 4)
    in_n = local(n_hbm, nv, 5)
    in_down = local(down_hbm, down, 6)
    in_up = local(up_hbm, up, 7)
    in_len = local(len_hbm, len_ref, 8)
    in_g = [
        local(
            g_hbm.at[:, pl.ds(h * HEAD, HEAD)],
            gv.at[h // 2, pl.ds((h % 2) * B, B), :],
            9 + h,
        )
        for h in range(2 * pairs)
    ]
    due = {"k": in_k, "q": [in_q, in_len], "n": [in_n, in_down], "w": [in_codes, in_scales]}
    due.update({"g": in_g, "up": [in_up]})
    for group in ("k", "q", "n", "w", "g", "up"):
        for c in due[group]:
            c.start()

    def ready(group):
        for c in due.pop(group):
            c.wait()

    sent = []
    coming = {}

    def send(copies, group=None):
        for c in copies:
            c.start()
        sent.extend(copies)
        if group:
            coming[group] = copies

    def arrive(group):
        for c in coming.pop(group):
            c.wait_recv()

    barrier = pltpu.get_barrier_semaphore()

    def greet(axis, me, size):
        def one(k, carry):
            pl.semaphore_signal(
                barrier, inc=1, device_id={axis: lax.rem(me + k, size)}, device_id_type=MESH
            )
            return carry
        lax.fori_loop(1, size, one, 0)

    for k in tree.near:
        for away in (k, S - k):
            pl.semaphore_signal(
                barrier, inc=1, device_id={"seq": lax.rem(seq + away, S)}, device_id_type=MESH
            )
    greet("tensor", ten, T)
    greet("dp", dp, D)
    greeted = 2 * len(tree.near) + T + D - 2
    if tree.far:
        owner_there = lax.rem(seq - tree.far + S, S)

        @pl.when(owner_there + tree.least[tree.far] <= last)
        def _():
            pl.semaphore_signal(barrier, inc=1, device_id={"seq": owner_there}, device_id_type=MESH)

        greeted = greeted + (seq + tree.least[tree.far] <= last).astype(jnp.int32)

    def k_copy(a, b, where):
        return remote(kbuf.at[a], kbuf.at[b], k_send.at[b], k_recv.at[b], {"seq": where})

    def runs(b):
        return lax.rem(seq - b + S, S) + tree.least[b] <= last

    def pass_down(a):
        for b in tree.children[a]:
            @pl.when(lax.rem(seq - a + S, S) + tree.least[b] <= last)
            def _(b=b):
                k_copy(a, b, lax.rem(seq + b - a + S, S)).start()

    def k_arrive(b):
        k_copy(0, b, seq).wait_recv()

    ready("q")
    ready("k")
    ipos = seq * B + lax.broadcasted_iota(jnp.int32, (1, B), 1)
    start = jnp.zeros((1, B), jnp.int32)
    bound = jnp.int32(0)
    for d in range(len_ref.shape[1] - 1):
        bound = bound + len_ref[0, d]
        start = jnp.where(ipos >= bound, bound, start)
    jrow = lax.broadcasted_iota(jnp.int32, (B, B), 0)
    scale = math.log2(math.e) / math.sqrt(HEAD)

    for h in range(2 * pairs):
        qt[h // 2, :, (h % 2) * B : (h % 2 + 1) * B] = qv[:, h * HEAD : (h + 1) * HEAD].T
    m_ref[...] = jnp.full(m_ref.shape, NEG, F32)
    l_ref[...] = jnp.zeros(l_ref.shape, F32)

    def attend(slot):
        jpos = lax.rem(seq - slot + S, S) * B + jrow
        allowed = (jpos >= start) & (jpos <= ipos)
        bias = jnp.where(allowed, 0.0, NEG).astype(F32)
        bias_ref[...] = jnp.concatenate([bias, bias], axis=1)

        for hp in range(pairs):
            x = dot(kbuf[slot, hp // per_kv], qt[hp]) * scale + bias_ref[...]
            old = m_ref[hp]
            new = jnp.maximum(old, jnp.max(x, axis=0, keepdims=True))
            w = jnp.exp2(x - new)
            l_ref[hp] = l_ref[hp] * jnp.exp2(old - new) + jnp.sum(w, axis=0, keepdims=True)
            w_ref[slot, hp] = w.astype(BF16)
            m_ref[hp] = new
            ms_ref[slot, hp] = new

    def attend_on_arrival(slot):
        @pl.when(seq >= slot)
        def _():
            k_arrive(slot)
            attend(slot)

    attend(0)
    pl.semaphore_wait(barrier, greeted)
    pass_down(0)

    ready("n")
    xa_buf[0] = dot_general(down[...], nv[...], NT).astype(BF16)

    def xa_copy(k):
        return remote(
            xa_buf.at[0], xa_buf.at[k], xa_send.at[k], xa_recv.at[k], {"tensor": lax.rem(ten + k, T)}
        )

    send([xa_copy(k) for k in range(1, T)], "xa")

    ready("w")

    def dequantised(first, n, put):
        def one(i, carry):
            row = pl.multiple_of(first + i * GROUP, GROUP)
            block = codes[pl.ds(row, GROUP), :].astype(F32)
            put(i, (block * scales[pl.ds(lax.div(row, GROUP), 1), :]).astype(BF16))
            return carry
        lax.fori_loop(0, n // GROUP, one, 0)

    def w_copy(k):
        return remote(
            wst.at[k], wfull.at[k, core], w_send.at[k], w_recv.at[k], {"tensor": lax.rem(ten + k, T)}
        )

    def wc_copy(k, h):
        return remote(wfull.at[k, h], wfull.at[k, h], wc_send.at[k], wc_recv.at[k], {"dp": sibling})

    def send_weights(k):
        def put(i, value):
            wst[k, pl.ds(pl.multiple_of(i * GROUP, GROUP), GROUP), :] = value
        dequantised(lax.rem(ten + k, T) * feats + core * hf, hf, put)
        send([w_copy(k)])

    def own_weights():
        for h in range(2):
            def put(i, value, h=h):
                wfull[0, h, pl.ds(pl.multiple_of(i * GROUP, GROUP), GROUP), :] = value
            dequantised(ten * feats + h * hf, hf, put)


    for n, a in enumerate(tree.relays):
        @pl.when(runs(a))
        def _(a=a):
            k_arrive(a)
            pass_down(a)
        if n + 1 < T:
            send_weights(n + 1)
        for b in tree.after[a]:
            if b in tree.relays:
                @pl.when(seq >= b)
                def _(b=b):
                    attend(b)
            else:
                attend_on_arrival(b)
    for k in range(len(tree.relays) + 1, T):
        send_weights(k)
    coming["w"] = [w_copy(k) for k in range(1, T)]
    for b in tree.final:
        attend_on_arrival(b)

    l_ref[...] = 1.0 / l_ref[...]
    ready("g")

    def partial(slot):
        for g in range(KV):
            total = None
            for i in range(per_kv):
                hp = g * per_kv + i
                factor = jnp.exp2(ms_ref[slot, hp] - m_ref[hp]) * l_ref[hp]
                p = (w_ref[slot, hp].astype(F32) * factor).astype(BF16)
                one = dot(p, gv[hp])
                total = one if total is None else total + one
            acc_ref[g] = total

    def s_copy(a, b, where):
        return remote(rs_out.at[b], rs_in.at[b], s_send.at[b], s_recv.at[b], {"seq": where})

    def up_to(a, b):
        return s_copy(a, b, lax.rem(seq + a - b + S, S))

    def gather(a, keep):
        if a == 0:
            partial(0)
        else:
            @pl.when(seq >= a)
            def _():
                partial(a)

            @pl.when(seq < a)
            def _():
                acc_ref[...] = jnp.zeros(acc_ref.shape, F32)
        for b in tree.children[a]:
            @pl.when(lax.rem(seq - a + S, S) + tree.least[b] <= last)
            def _(b=b):
                s_copy(a, b, seq).wait_recv()
                acc_ref[...] += rs_in[b].astype(F32)
        if keep:
            rs_out[a] = acc_ref[...].astype(BF16)

    for b in tree.up:
        @pl.when(runs(b))
        def _(b=b):
            gather(b, True)
            up_to(tree.parent[b], b).start()

    arrive("xa")
    xat = xa_buf[0].astype(F32)
    for k in range(1, T):
        xat = xat + xa_buf[k].astype(F32)
    xat = xat.astype(BF16)
    arrive("w")
    send([wc_copy(k, core) for k in range(1, T)])
    coming["wc"] = [wc_copy(k, 1 - core) for k in range(1, T)]
    ready("up")
    gather(0, False)
    for g in range(KV):
        dv_buf[0, :, g * HEAD : (g + 1) * HEAD] = acc_ref[g].astype(BF16)

    dv = dv_buf[0]
    gx_buf[0] = dot_general(up[...], dv, NT).astype(BF16)

    def gx_copy(k):
        return remote(
            gx_buf.at[0], gx_buf.at[k], gx_send.at[k], gx_recv.at[k], {"tensor": lax.rem(ten + k, T)}
        )

    def dv_copy(k):
        return remote(
            dv_buf.at[0], dv_buf.at[k], dv_send.at[k], dv_recv.at[k], {"tensor": lax.rem(ten + k, T)}
        )

    send([gx_copy(k) for k in range(1, T)], "gx")
    send([dv_copy(k) for k in range(1, T)], "dv")
    per = a_src.shape[1]
    across = (feats + cols) // 128

    def tile_at(i, j):
        n = i * across + j
        return n // per, n % per

    part_b = dot(xat, dv)
    for i in range(rank // 16):
        for j in range(cols // 128):
            p, q = tile_at(i, feats // 128 + j)
            a_src[p, q] = part_b[i * 16 : i * 16 + 16, j * 128 : j * 128 + 128].astype(BF16)
    arrive("gx")
    gpt = gx_buf[0].astype(F32)
    for k in range(1, T):
        gpt = gpt + gx_buf[k].astype(F32)
    gpt = gpt.astype(BF16)
    for j in range(feats // 128):
        part_a = dot(gpt, nv[:, j * 128 : j * 128 + 128])
        for i in range(rank // 16):
            p, q = tile_at(i, j)
            a_src[p, q] = part_a[i * 16 : i * 16 + 16].astype(BF16)

    def a_copy(k):
        peer = lax.rem(dp + k, D)
        return remote(a_src.at[peer], a_rcv.at[k], a_send.at[k], a_recv.at[k], {"dp": peer})

    send([a_copy(k) for k in range(1, D)], "a")
    own_weights()
    arrive("a")
    total = a_src[dp].astype(F32)
    for k in range(1, D):
        total = total + a_rcv[k].astype(F32)
    b_src[...] = total.astype(BF16)

    owners = [j * S // per for j in range(per)]

    def b_copy(j):
        away = lax.rem(owners[j] - seq + S, S)
        return remote(
            b_src.at[j], b_rcv.at[away], b_send.at[j], b_recv.at[away], {"seq": jnp.int32(owners[j])}
        )

    mine = jnp.int32(0)
    owner = seq == owners[0]
    for j in range(1, per):
        mine = jnp.where(seq == owners[j], j, mine)
        owner = owner | (seq == owners[j])

    for j in range(per):
        @pl.when(seq != owners[j])
        def _():
            b_copy(j).start()

    def c_copy(k):
        return remote(
            c_buf.at[mine], c_buf.at[mine], c_send.at[k], c_recv.at[mine], {"seq": lax.rem(seq + k, S)}
        )

    @pl.when(owner)
    def _():
        total = b_src[mine].astype(F32)
        for k in range(1, S):
            remote(
                b_src.at[0], b_rcv.at[k], b_send.at[0], b_recv.at[k], {"seq": lax.rem(seq + k, S)}
            ).wait_recv()
            total = total + b_rcv[k].astype(F32)
        c_buf[mine] = total.astype(BF16)
        for k in range(1, S):
            c_copy(k).start()

    for j in range(per):
        @pl.when(seq != owners[j])
        def _():
            remote(
                b_src.at[j], c_buf.at[j], c_send.at[0], c_recv.at[j], {"seq": jnp.int32(owners[j])}
            ).wait_recv()

    def d_copy(k):
        return remote(
            c_buf, d_buf.at[dp], d_send.at[k], d_recv.at[dp], {"dp": lax.rem(dp + k, D)}
        )

    send([d_copy(k) for k in range(1, D)])

    def d_from(k):
        peer = lax.rem(dp + k, D)
        return remote(c_buf, d_buf.at[peer], d_send.at[k], d_recv.at[peer], {"dp": peer})

    coming["d"] = [d_from(k) for k in range(1, D)]
    d_buf[dp] = c_buf[...]

    gp = gpt.T
    arrive("dv")
    arrive("wc")
    width = min(256, hf)
    for n in range(feats // width):
        h, row = n * width // hf, n * width % hf
        at = slice(n * width, (n + 1) * width)
        total = 2.0 * dot(gp, down[:, at])
        for k in range(T):
            total = total + dot_general(dv_buf[k], wfull[k, h, row : row + width, :], NT)
        dn_ref[:, at] = total.astype(BF16)

    arrive("d")
    factor = 2.0 / math.sqrt(D * S * B)
    for i in range(rank // 16):
        for j in range(across):
            p, q = tile_at(i, j)
            value = d_buf[p, q].astype(F32) * factor
            if j < feats // 128:
                ga_ref[i * 16 : i * 16 + 16, j * 128 : j * 128 + 128] = value
            else:
                c = j * 128 - feats
                gb_ref[i * 16 : i * 16 + 16, c : c + 128] = value

    for c in sent:
        c.wait_send()
    for b, a in tree.parent.items():

        @pl.when(lax.rem(seq - a + S, S) + tree.least[b] <= last)
        def _(a=a, b=b):
            k_copy(a, b, seq).wait_send()

        @pl.when(runs(b))
        def _(b=b):
            up_to(a, b).wait_send()
    for j in range(per):
        @pl.when(seq != owners[j])
        def _():
            b_copy(j).wait_send()

    @pl.when(owner)
    def _():
        for k in range(1, S):
            c_copy(k).wait_send()


def body(
    shape, queries, keys, output_gradient, normed, document_length, codes, scales,
    adapter_down, adapter_up,
):
    D, S, T = shape
    B = queries.shape[1]
    heads = queries.shape[2] // HEAD
    pairs = heads // 2
    feats = normed.shape[2]
    rank, cols = adapter_up.shape
    per = (rank // 16) * ((feats + cols) // 128) // D
    hbm = pl.BlockSpec(memory_space=pltpu.HBM)
    vmem = pl.BlockSpec(memory_space=pltpu.VMEM)
    dma = pltpu.SemaphoreType.DMA
    d_normed, grad_a, grad_b = pl.pallas_call(
        functools.partial(kernel, shape),
        out_shape=(
            jax.ShapeDtypeStruct((B, feats), BF16),
            jax.ShapeDtypeStruct((rank, feats), F32),
            jax.ShapeDtypeStruct((rank, cols), F32),
        ),
        in_specs=[hbm] * 9,
        out_specs=(vmem, vmem, vmem),
        scratch_shapes=[
            pltpu.SMEM(document_length.shape, jnp.int32),
            pltpu.VMEM((S, KV, B, HEAD), BF16),
            pltpu.VMEM((B, heads * HEAD), BF16),
            pltpu.VMEM((pairs, HEAD, 2 * B), BF16),
            pltpu.VMEM((pairs, 2 * B, HEAD), BF16),
            pltpu.VMEM((B, feats), BF16),
            pltpu.VMEM(codes.shape, BF16),
            pltpu.VMEM(scales.shape, F32),
            pltpu.VMEM((rank, feats), BF16),
            pltpu.VMEM((rank, cols), BF16),
            pltpu.VMEM((T, feats // 2, cols), BF16),
            pltpu.VMEM((T, 2, feats // 2, cols), BF16),
            pltpu.VMEM((B, 2 * B), F32),
            pltpu.VMEM((pairs, 1, 2 * B), F32),
            pltpu.VMEM((pairs, 1, 2 * B), F32),
            pltpu.VMEM((S, pairs, 1, 2 * B), F32),
            pltpu.VMEM((S, pairs, B, 2 * B), BF16),
            pltpu.VMEM((KV, B, HEAD), F32),
            pltpu.VMEM((S, KV, B, HEAD), BF16),
            pltpu.VMEM((S, KV, B, HEAD), BF16),
            pltpu.VMEM((T, rank, B), BF16),
            pltpu.VMEM((T, rank, B), BF16),
            pltpu.VMEM((T, B, cols), BF16),
            pltpu.VMEM((D, per, 16, 128), BF16),
            pltpu.VMEM((D, per, 16, 128), BF16),
            pltpu.VMEM((per, 16, 128), BF16),
            pltpu.VMEM((S, 16, 128), BF16),
            pltpu.VMEM((per, 16, 128), BF16),
            pltpu.VMEM((D, per, 16, 128), BF16),
            dma((9 + heads,)),
            dma((S,)),
            dma((S,)),
            dma((S,)),
            dma((S,)),
            dma((T,)),
            dma((T,)),
            dma((T,)),
            dma((T,)),
            dma((T,)),
            dma((T,)),
            dma((T,)),
            dma((T,)),
            dma((T,)),
            dma((T,)),
            dma((D,)),
            dma((D,)),
            dma((per,)),
            dma((S,)),
            dma((S,)),
            dma((per,)),
            dma((D,)),
            dma((D,)),
        ],
        compiler_params=pltpu.CompilerParams(
            collective_id=0, has_side_effects=True, vmem_limit_bytes=40 * 1024 * 1024
        ),
        name="value_backward",
    )(
        *(
            pltpu.with_memory_space_constraint(x, pltpu.HBM)
            for x in (
                queries[0], keys[0], output_gradient[0], normed[0], document_length, codes,
                scales, adapter_down.T, adapter_up,
            )
        )
    )
    return d_normed[None], grad_a.T, grad_b


def solution(mesh):
    shape = tuple(mesh.shape[a] for a in ("dp", "seq", "tensor"))
    split = P("dp", "seq", "tensor")
    placed = (
        split, split, split, split,
        P("dp", None), P(None, "tensor"), P(None, "tensor"), P("tensor", None), P(None, "tensor"),
    )
    return jax.shard_map(
        functools.partial(body, shape),
        mesh=mesh,
        in_specs=placed,
        out_specs=(split, P("tensor", None), P(None, "tensor")),
        check_vma=False,
    )
```

```python
import functools
import math

import jax
import jax.numpy as jnp
from jax import lax
from jax.experimental import pallas as pl
from jax.experimental.pallas import tpu as pltpu
from jax.sharding import PartitionSpec as P

MESH = pl.DeviceIdType.MESH
HEAD = 128
GROUP = 128
KV = 2
QUAD = 4
NEG = -1e30
F32 = jnp.float32
BF16 = jnp.bfloat16
NT = (((1,), (1,)), ((), ()))
TN = (((0,), (0,)), ((), ()))


def dot(a, b):
    return jnp.dot(a, b, preferred_element_type=F32)


def dot_general(a, b, dims):
    return lax.dot_general(a, b, dims, preferred_element_type=F32)


class Tree:
    def __init__(self, size):
        if size == 16:
            self.parent = {3: 0, 1: 0, 13: 0, 6: 3, 2: 3, 11: 13, 12: 13, 10: 11, 9: 11}
            self.parent.update({8: 6, 4: 6, 7: 6, 5: 6})
            self.after = {3: [], 13: [3, 1], 11: [11, 2], 6: [6]}
            self.final = [12, 10, 9, 7, 5, 8, 4]
            self.up = [8, 4, 7, 5, 10, 9, 12, 2, 1, 6, 11, 3, 13]
            self.passing = [13]
        else:
            self.parent = {b: b - 1 for b in range(1, size)}
            self.after = {b: [b] for b in range(1, size - 1)}
            self.final = [size - 1]
            self.up = list(range(size - 1, 0, -1))
            self.passing = []
        self.near = [k for k in (1, 2, 3) if 2 * k <= size]
        self.relays = list(self.after)
        self.children = {a: [b for b in self.parent if self.parent[b] == a] for a in range(size)}
        self.least = {b: min(x for x in self.below(b) if x not in self.passing) for b in self.parent}

    def below(self, b):
        return [b] + [x for child in self.children[b] for x in self.below(child)]


def kernel(
    shape,
    q_hbm, k_hbm, g_hbm, n_hbm, len_hbm, codes_hbm, scales_hbm, down_hbm, up_hbm,
    dn_ref, ga_ref, gb_ref,
    len_ref, kbuf, qv, qt, gv, nv, codes, scales, down, up, wst, wfull, bias_ref,
    m_ref, l_ref, ms_ref, w_ref, acc_ref, rs_out, rs_in, xa_buf, gx_buf, dv_buf,
    a_src, a_rcv, b_buf, c_buf, d_buf,
    met_sem, local_sem, k_send, k_recv, s_send, s_recv,
    w_send, w_recv, wc_send, wc_recv, xa_send, xa_recv, gx_send, gx_recv,
    dv_send, dv_recv, a_send, a_recv, b_send, b_recv, d_send, d_recv,
):
    D, S, T = shape
    tree = Tree(S)
    B = kbuf.shape[2]
    pairs = qt.shape[0]
    per_kv = pairs // KV
    feats = nv.shape[1]
    rank = up.shape[0]
    cols = up.shape[1]
    hf = feats // 2
    dp = lax.axis_index("dp")
    seq = lax.axis_index("seq")
    ten = lax.axis_index("tensor")
    core = lax.rem(dp, 2)
    sibling = dp + 1 - 2 * core
    last = S - 1

    def remote(src, dst, send, recv, where):
        return pltpu.make_async_remote_copy(
            src_ref=src, dst_ref=dst, send_sem=send, recv_sem=recv,
            device_id=where, device_id_type=MESH,
        )

    def local(src, dst, i):
        return pltpu.make_async_copy(src, dst, local_sem.at[i])

    in_k = [local(k_hbm.at[:, pl.ds(g * HEAD, HEAD)], kbuf.at[0, g], g) for g in range(KV)]
    in_q = local(q_hbm, qv, 2)
    in_codes = local(codes_hbm, codes, 3)
    in_scales = local(scales_hbm, scales, 4)
    in_n = local(n_hbm, nv, 5)
    in_down = local(down_hbm, down, 6)
    in_up = local(up_hbm, up, 7)
    in_len = local(len_hbm, len_ref, 8)
    in_g = [
        local(
            g_hbm.at[:, pl.ds(h * HEAD, HEAD)],
            gv.at[h // 2, pl.ds((h % 2) * B, B), :],
            9 + h,
        )
        for h in range(2 * pairs)
    ]
    due = {"k": in_k, "q": [in_q, in_len], "n": [in_n, in_down], "w": [in_codes, in_scales]}
    due.update({"g": in_g, "up": [in_up]})
    for group in ("k", "q", "n", "w", "g", "up"):
        for c in due[group]:
            c.start()

    def ready(group):
        for c in due.pop(group):
            c.wait()

    sent = []
    coming = {}

    def send(copies, group=None):
        for c in copies:
            c.start()
        sent.extend(copies)
        if group:
            coming[group] = copies

    def arrive(group):
        for c in coming.pop(group):
            c.wait_recv()

    barrier = pltpu.get_barrier_semaphore()

    def greet(axis, me, size):
        def one(k, carry):
            pl.semaphore_signal(
                barrier, inc=1, device_id={axis: lax.rem(me + k, size)}, device_id_type=MESH
            )
            return carry
        lax.fori_loop(1, size, one, 0)

    for k in tree.near:
        for away in (k, S - k):
            pl.semaphore_signal(
                barrier, inc=1, device_id={"seq": lax.rem(seq + away, S)}, device_id_type=MESH
            )
    greet("tensor", ten, T)
    greet("dp", dp, D)
    greeted = 2 * len(tree.near) + T + D - 2
    def k_copy(a, b, where):
        return remote(kbuf.at[a], kbuf.at[b], k_send.at[b], k_recv.at[b], {"seq": where})

    def runs(b):
        return lax.rem(seq - b + S, S) + tree.least[b] <= last

    def pass_down(a):
        for b in tree.children[a]:
            @pl.when(lax.rem(seq - a + S, S) + tree.least[b] <= last)
            def _(b=b):
                k_copy(a, b, lax.rem(seq + b - a + S, S)).start()

    def k_arrive(b):
        k_copy(0, b, seq).wait_recv()

    ready("q")
    ready("k")
    ipos = seq * B + lax.broadcasted_iota(jnp.int32, (1, B), 1)
    start = jnp.zeros((1, B), jnp.int32)
    bound = jnp.int32(0)
    for d in range(len_ref.shape[1] - 1):
        bound = bound + len_ref[0, d]
        start = jnp.where(ipos >= bound, bound, start)
    jrow = lax.broadcasted_iota(jnp.int32, (B, B), 0)
    scale = math.log2(math.e) / math.sqrt(HEAD)

    for h in range(2 * pairs):
        qt[h // 2, :, (h % 2) * B : (h % 2 + 1) * B] = qv[:, h * HEAD : (h + 1) * HEAD].T
    m_ref[...] = jnp.full(m_ref.shape, NEG, F32)
    l_ref[...] = jnp.zeros(l_ref.shape, F32)

    def attend(slot):
        jpos = lax.rem(seq - slot + S, S) * B + jrow
        allowed = (jpos >= start) & (jpos <= ipos)
        bias = jnp.where(allowed, 0.0, NEG).astype(F32)
        bias_ref[...] = jnp.concatenate([bias, bias], axis=1)

        for hp in range(pairs):
            x = dot(kbuf[slot, hp // per_kv], qt[hp]) * scale + bias_ref[...]
            old = m_ref[hp]
            new = jnp.maximum(old, jnp.max(x, axis=0, keepdims=True))
            w = jnp.exp2(x - new)
            l_ref[hp] = l_ref[hp] * jnp.exp2(old - new) + jnp.sum(w, axis=0, keepdims=True)
            w_ref[slot, hp] = w.astype(BF16)
            m_ref[hp] = new
            ms_ref[slot, hp] = new

    def attend_on_arrival(slot):
        @pl.when(seq >= slot)
        def _():
            k_arrive(slot)
            attend(slot)

    attend(0)
    pl.semaphore_wait(barrier, greeted)
    pass_down(0)
    for k in range(1, D):
        pl.semaphore_signal(
            met_sem, inc=1, device_id={"dp": lax.rem(dp + k, D)}, device_id_type=MESH
        )

    ready("n")
    xa_buf[0] = dot_general(down[...], nv[...], NT).astype(BF16)

    def xa_copy(k):
        return remote(
            xa_buf.at[0], xa_buf.at[k], xa_send.at[k], xa_recv.at[k], {"tensor": lax.rem(ten + k, T)}
        )

    send([xa_copy(k) for k in range(1, T)], "xa")

    ready("w")

    def dequantised(first, n, put):
        def one(i, carry):
            row = pl.multiple_of(first + i * GROUP, GROUP)
            block = codes[pl.ds(row, GROUP), :].astype(F32)
            put(i, (block * scales[pl.ds(lax.div(row, GROUP), 1), :]).astype(BF16))
            return carry
        lax.fori_loop(0, n // GROUP, one, 0)

    def w_copy(k):
        return remote(
            wst.at[k], wfull.at[k, core], w_send.at[k], w_recv.at[k], {"tensor": lax.rem(ten + k, T)}
        )

    def wc_copy(k, h):
        return remote(wfull.at[k, h], wfull.at[k, h], wc_send.at[k], wc_recv.at[k], {"dp": sibling})

    def send_weights(k):
        def put(i, value):
            wst[k, pl.ds(pl.multiple_of(i * GROUP, GROUP), GROUP), :] = value
        dequantised(lax.rem(ten + k, T) * feats + core * hf, hf, put)
        send([w_copy(k)])

    def own_weights():
        for h in range(2):
            def put(i, value, h=h):
                wfull[0, h, pl.ds(pl.multiple_of(i * GROUP, GROUP), GROUP), :] = value
            dequantised(ten * feats + h * hf, hf, put)


    for n, a in enumerate(tree.relays):
        @pl.when(runs(a))
        def _(a=a):
            k_arrive(a)
            pass_down(a)
        if n + 1 < T:
            send_weights(n + 1)
        for b in tree.after[a]:
            if b in tree.relays:
                @pl.when(seq >= b)
                def _(b=b):
                    attend(b)
            else:
                attend_on_arrival(b)
    for k in range(len(tree.relays) + 1, T):
        send_weights(k)
    coming["w"] = [w_copy(k) for k in range(1, T)]
    for b in tree.final:
        attend_on_arrival(b)

    l_ref[...] = 1.0 / l_ref[...]
    ready("g")

    def partial(slot):
        for g in range(KV):
            total = None
            for i in range(per_kv):
                hp = g * per_kv + i
                factor = jnp.exp2(ms_ref[slot, hp] - m_ref[hp]) * l_ref[hp]
                p = (w_ref[slot, hp].astype(F32) * factor).astype(BF16)
                one = dot(p, gv[hp])
                total = one if total is None else total + one
            acc_ref[g] = total

    def s_copy(a, b, where):
        return remote(rs_out.at[b], rs_in.at[b], s_send.at[b], s_recv.at[b], {"seq": where})

    def up_to(a, b):
        return s_copy(a, b, lax.rem(seq + a - b + S, S))

    def gather(a, keep):
        if a == 0:
            partial(0)
        elif a in tree.passing:
            acc_ref[...] = jnp.zeros(acc_ref.shape, F32)
        else:
            @pl.when(seq >= a)
            def _():
                partial(a)

            @pl.when(seq < a)
            def _():
                acc_ref[...] = jnp.zeros(acc_ref.shape, F32)
        for b in tree.children[a]:
            @pl.when(lax.rem(seq - a + S, S) + tree.least[b] <= last)
            def _(b=b):
                s_copy(a, b, seq).wait_recv()
                acc_ref[...] += rs_in[b].astype(F32)
        if keep:
            rs_out[a] = acc_ref[...].astype(BF16)

    for b in tree.up:
        @pl.when(runs(b))
        def _(b=b):
            gather(b, True)
            up_to(tree.parent[b], b).start()

    arrive("xa")
    xat = xa_buf[0].astype(F32)
    for k in range(1, T):
        xat = xat + xa_buf[k].astype(F32)
    xat = xat.astype(BF16)
    arrive("w")
    send([wc_copy(k, core) for k in range(1, T)])
    coming["wc"] = [wc_copy(k, 1 - core) for k in range(1, T)]
    ready("up")
    gather(0, False)
    for g in range(KV):
        dv_buf[0, :, g * HEAD : (g + 1) * HEAD] = acc_ref[g].astype(BF16)

    dv = dv_buf[0]
    gx_buf[0] = dot_general(up[...], dv, NT).astype(BF16)

    def gx_copy(k):
        return remote(
            gx_buf.at[0], gx_buf.at[k], gx_send.at[k], gx_recv.at[k], {"tensor": lax.rem(ten + k, T)}
        )

    def dv_copy(k):
        return remote(
            dv_buf.at[0], dv_buf.at[k], dv_send.at[k], dv_recv.at[k], {"tensor": lax.rem(ten + k, T)}
        )

    send([gx_copy(k) for k in range(1, T)], "gx")
    send([dv_copy(k) for k in range(1, T)], "dv")
    members = D * QUAD
    quads = S // QUAD
    place = lax.rem(seq, QUAD)
    quad = lax.div(seq, QUAD)
    mine = dp * QUAD + place
    wide_a = feats // 128
    wide_b = cols // 128
    n_tiles = (rank // 16) * (wide_a + wide_b)

    def tile_a(i, j):
        n = i * wide_a + j
        return n % members, n // members

    def tile_b(i, j):
        n = (rank // 16) * wide_a + i * wide_b + j
        return n % members, n // members

    for n in range(n_tiles, members * a_src.shape[1]):
        a_src[n % members, n // members] = jnp.zeros((16, 128), BF16)
    part_b = dot(xat, dv)
    for i in range(rank // 16):
        for j in range(cols // 128):
            p, q = tile_b(i, j)
            a_src[p, q] = part_b[i * 16 : i * 16 + 16, j * 128 : j * 128 + 128].astype(BF16)
    arrive("gx")
    gpt = gx_buf[0].astype(F32)
    for k in range(1, T):
        gpt = gpt + gx_buf[k].astype(F32)
    gpt = gpt.astype(BF16)
    for j in range(feats // 128):
        part_a = dot(gpt, nv[:, j * 128 : j * 128 + 128])
        for i in range(rank // 16):
            p, q = tile_a(i, j)
            a_src[p, q] = part_a[i * 16 : i * 16 + 16].astype(BF16)

    def member(k):
        there = lax.rem(dp + lax.div(k, QUAD), D)
        at = lax.rem(place + lax.rem(k, QUAD), QUAD)
        return there * QUAD + at, {"dp": there, "seq": quad * QUAD + at}

    def a_copy(k):
        piece, where = member(k)
        return remote(a_src.at[piece], a_rcv.at[k], a_send.at[k], a_recv.at[k], where)

    def each(first, end, act):
        def one(k, carry):
            act(k)
            return carry
        lax.fori_loop(first, end, one, 0)

    pl.semaphore_wait(met_sem, D - 1)
    each(1, members, lambda k: a_copy(k).start())
    own_weights()

    def add(k, total):
        a_copy(k).wait_recv()
        return total + a_rcv[k].astype(F32)

    b_buf[quad] = lax.fori_loop(1, members, add, a_src[mine].astype(F32)).astype(BF16)

    def b_copy(j):
        there = lax.rem(quad + j, quads)
        return remote(
            b_buf.at[quad], b_buf.at[quad], b_send.at[j], b_recv.at[quad],
            {"seq": there * QUAD + place},
        )

    def b_from(j):
        there = lax.rem(quad + j, quads)
        return remote(
            b_buf.at[there], b_buf.at[there], b_send.at[j], b_recv.at[there],
            {"seq": there * QUAD + place},
        )

    send([b_copy(j) for j in range(1, quads)])
    for j in range(1, quads):
        b_from(j).wait_recv()
    total = b_buf[0].astype(F32)
    for j in range(1, quads):
        total = total + b_buf[j].astype(F32)
    c_buf[...] = total.astype(BF16)

    def d_copy(k):
        where = member(k)[1]
        return remote(c_buf, d_buf.at[mine], d_send.at[k], d_recv.at[mine], where)

    def d_from(k):
        piece, where = member(k)
        return remote(c_buf, d_buf.at[piece], d_send.at[k], d_recv.at[piece], where)

    each(1, members, lambda k: d_copy(k).start())
    d_buf[mine] = c_buf[...]

    gp = gpt.T
    arrive("dv")
    arrive("wc")
    width = min(256, hf)
    for n in range(feats // width):
        h, row = n * width // hf, n * width % hf
        at = slice(n * width, (n + 1) * width)
        total = 2.0 * dot(gp, down[:, at])
        for k in range(T):
            total = total + dot_general(dv_buf[k], wfull[k, h, row : row + width, :], NT)
        dn_ref[:, at] = total.astype(BF16)

    each(1, members, lambda k: d_from(k).wait_recv())
    factor = 2.0 / math.sqrt(D * S * B)
    for i in range(rank // 16):
        at = slice(i * 16, i * 16 + 16)
        for j in range(wide_a):
            ga_ref[at, j * 128 : j * 128 + 128] = d_buf[tile_a(i, j)].astype(F32) * factor
        for j in range(wide_b):
            gb_ref[at, j * 128 : j * 128 + 128] = d_buf[tile_b(i, j)].astype(F32) * factor

    for c in sent:
        c.wait_send()
    for b, a in tree.parent.items():

        @pl.when(lax.rem(seq - a + S, S) + tree.least[b] <= last)
        def _(a=a, b=b):
            k_copy(a, b, seq).wait_send()

        @pl.when(runs(b))
        def _(b=b):
            up_to(a, b).wait_send()
    each(1, members, lambda k: a_copy(k).wait_send())
    each(1, members, lambda k: d_copy(k).wait_send())


def body(
    shape, queries, keys, output_gradient, normed, document_length, codes, scales,
    adapter_down, adapter_up,
):
    D, S, T = shape
    B = queries.shape[1]
    heads = queries.shape[2] // HEAD
    pairs = heads // 2
    feats = normed.shape[2]
    rank, cols = adapter_up.shape
    members = D * QUAD
    per = -(-(rank // 16) * ((feats + cols) // 128) // members)
    hbm = pl.BlockSpec(memory_space=pltpu.HBM)
    vmem = pl.BlockSpec(memory_space=pltpu.VMEM)
    dma = pltpu.SemaphoreType.DMA
    d_normed, grad_a, grad_b = pl.pallas_call(
        functools.partial(kernel, shape),
        out_shape=(
            jax.ShapeDtypeStruct((B, feats), BF16),
            jax.ShapeDtypeStruct((rank, feats), F32),
            jax.ShapeDtypeStruct((rank, cols), F32),
        ),
        in_specs=[hbm] * 9,
        out_specs=(vmem, vmem, vmem),
        scratch_shapes=[
            pltpu.SMEM(document_length.shape, jnp.int32),
            pltpu.VMEM((S, KV, B, HEAD), BF16),
            pltpu.VMEM((B, heads * HEAD), BF16),
            pltpu.VMEM((pairs, HEAD, 2 * B), BF16),
            pltpu.VMEM((pairs, 2 * B, HEAD), BF16),
            pltpu.VMEM((B, feats), BF16),
            pltpu.VMEM(codes.shape, BF16),
            pltpu.VMEM(scales.shape, F32),
            pltpu.VMEM((rank, feats), BF16),
            pltpu.VMEM((rank, cols), BF16),
            pltpu.VMEM((T, feats // 2, cols), BF16),
            pltpu.VMEM((T, 2, feats // 2, cols), BF16),
            pltpu.VMEM((B, 2 * B), F32),
            pltpu.VMEM((pairs, 1, 2 * B), F32),
            pltpu.VMEM((pairs, 1, 2 * B), F32),
            pltpu.VMEM((S, pairs, 1, 2 * B), F32),
            pltpu.VMEM((S, pairs, B, 2 * B), BF16),
            pltpu.VMEM((KV, B, HEAD), F32),
            pltpu.VMEM((S, KV, B, HEAD), BF16),
            pltpu.VMEM((S, KV, B, HEAD), BF16),
            pltpu.VMEM((T, rank, B), BF16),
            pltpu.VMEM((T, rank, B), BF16),
            pltpu.VMEM((T, B, cols), BF16),
            pltpu.VMEM((members, per, 16, 128), BF16),
            pltpu.VMEM((members, per, 16, 128), BF16),
            pltpu.VMEM((S // QUAD, per, 16, 128), BF16),
            pltpu.VMEM((per, 16, 128), BF16),
            pltpu.VMEM((members, per, 16, 128), BF16),
            pltpu.SemaphoreType.REGULAR,
            dma((9 + heads,)),
            dma((S,)),
            dma((S,)),
            dma((S,)),
            dma((S,)),
            dma((T,)),
            dma((T,)),
            dma((T,)),
            dma((T,)),
            dma((T,)),
            dma((T,)),
            dma((T,)),
            dma((T,)),
            dma((T,)),
            dma((T,)),
            dma((members,)),
            dma((members,)),
            dma((S // QUAD,)),
            dma((S // QUAD,)),
            dma((members,)),
            dma((members,)),
        ],
        compiler_params=pltpu.CompilerParams(
            collective_id=0, has_side_effects=True, vmem_limit_bytes=40 * 1024 * 1024
        ),
        name="value_backward",
    )(
        *(
            pltpu.with_memory_space_constraint(x, pltpu.HBM)
            for x in (
                queries[0], keys[0], output_gradient[0], normed[0], document_length, codes,
                scales, adapter_down.T, adapter_up,
            )
        )
    )
    return d_normed[None], grad_a.T, grad_b


def solution(mesh):
    shape = tuple(mesh.shape[a] for a in ("dp", "seq", "tensor"))
    split = P("dp", "seq", "tensor")
    placed = (
        split, split, split, split,
        P("dp", None), P(None, "tensor"), P(None, "tensor"), P("tensor", None), P(None, "tensor"),
    )
    return jax.shard_map(
        functools.partial(body, shape),
        mesh=mesh,
        in_specs=placed,
        out_specs=(split, P("tensor", None), P(None, "tensor")),
        check_vma=False,
    )
```

```python
import functools
import math

import jax
import jax.numpy as jnp
from jax import lax
from jax.experimental import pallas as pl
from jax.experimental.pallas import tpu as pltpu
from jax.sharding import PartitionSpec as P

MESH = pl.DeviceIdType.MESH
HEAD = 128
GROUP = 128
KV = 2
QUAD = 4
NEG = -1e30
F32 = jnp.float32
BF16 = jnp.bfloat16
NT = (((1,), (1,)), ((), ()))
TN = (((0,), (0,)), ((), ()))


def dot(a, b):
    return jnp.dot(a, b, preferred_element_type=F32)


def dot_general(a, b, dims):
    return lax.dot_general(a, b, dims, preferred_element_type=F32)


class Tree:
    def __init__(self, size):
        if size == 16:
            self.parent = {3: 0, 1: 0, 11: 0, 6: 3, 2: 3, 12: 11, 10: 11, 9: 11}
            self.parent.update({8: 6, 4: 6, 7: 6, 5: 6})
            self.after = {3: [], 11: [3, 1, 11], 6: [2, 6]}
            self.final = [12, 10, 9, 7, 5, 8, 4]
            self.up = [8, 4, 7, 5, 12, 10, 9, 2, 1, 6, 11, 3]
            self.far = 11
        else:
            self.parent = {b: b - 1 for b in range(1, size)}
            self.after = {b: [b] for b in range(1, size - 1)}
            self.final = [size - 1]
            self.up = list(range(size - 1, 0, -1))
            self.far = None
        self.near = [k for k in (1, 2, 3) if 2 * k <= size]
        self.relays = list(self.after)
        self.children = {a: [b for b in self.parent if self.parent[b] == a] for a in range(size)}
        self.least = {b: min(self.below(b)) for b in self.parent}

    def below(self, b):
        return [b] + [x for child in self.children[b] for x in self.below(child)]


def kernel(
    shape,
    q_hbm, k_hbm, g_hbm, n_hbm, len_hbm, codes_hbm, scales_hbm, down_hbm, up_hbm,
    dn_ref, ga_ref, gb_ref,
    len_ref, kbuf, qv, qt, gv, nv, codes, scales, down, up, wst, wfull, bias_ref,
    m_ref, l_ref, ms_ref, w_ref, acc_ref, rs_out, rs_in, xa_buf, gx_buf, dv_buf,
    a_src, a_rcv, b_buf, c_buf, d_buf,
    met_sem, local_sem, k_send, k_recv, s_send, s_recv,
    w_send, w_recv, wc_send, wc_recv, xa_send, xa_recv, gx_send, gx_recv,
    dv_send, dv_recv, a_send, a_recv, b_send, b_recv, d_send, d_recv,
):
    D, S, T = shape
    tree = Tree(S)
    B = kbuf.shape[2]
    pairs = qt.shape[0]
    per_kv = pairs // KV
    feats = nv.shape[1]
    rank = up.shape[0]
    cols = up.shape[1]
    hf = feats // 2
    dp = lax.axis_index("dp")
    seq = lax.axis_index("seq")
    ten = lax.axis_index("tensor")
    core = lax.rem(dp, 2)
    sibling = dp + 1 - 2 * core
    last = S - 1

    def remote(src, dst, send, recv, where):
        return pltpu.make_async_remote_copy(
            src_ref=src, dst_ref=dst, send_sem=send, recv_sem=recv,
            device_id=where, device_id_type=MESH,
        )

    def local(src, dst, i):
        return pltpu.make_async_copy(src, dst, local_sem.at[i])

    in_k = [local(k_hbm.at[:, pl.ds(g * HEAD, HEAD)], kbuf.at[0, g], g) for g in range(KV)]
    in_q = local(q_hbm, qv, 2)
    in_codes = local(codes_hbm, codes, 3)
    in_scales = local(scales_hbm, scales, 4)
    in_n = local(n_hbm, nv, 5)
    in_down = local(down_hbm, down, 6)
    in_up = local(up_hbm, up, 7)
    in_len = local(len_hbm, len_ref, 8)
    in_g = [
        local(
            g_hbm.at[:, pl.ds(h * HEAD, HEAD)],
            gv.at[h // 2, pl.ds((h % 2) * B, B), :],
            9 + h,
        )
        for h in range(2 * pairs)
    ]
    due = {"k": in_k, "q": [in_q, in_len], "n": [in_n, in_down], "w": [in_codes, in_scales]}
    due.update({"g": in_g, "up": [in_up]})
    for group in ("k", "q", "n", "w", "g", "up"):
        for c in due[group]:
            c.start()

    def ready(group):
        for c in due.pop(group):
            c.wait()

    sent = []
    coming = {}

    def send(copies, group=None):
        for c in copies:
            c.start()
        sent.extend(copies)
        if group:
            coming[group] = copies

    def arrive(group):
        for c in coming.pop(group):
            c.wait_recv()

    barrier = pltpu.get_barrier_semaphore()

    def greet(axis, me, size):
        def one(k, carry):
            pl.semaphore_signal(
                barrier, inc=1, device_id={axis: lax.rem(me + k, size)}, device_id_type=MESH
            )
            return carry
        lax.fori_loop(1, size, one, 0)

    for k in tree.near:
        for away in (k, S - k):
            pl.semaphore_signal(
                barrier, inc=1, device_id={"seq": lax.rem(seq + away, S)}, device_id_type=MESH
            )
    greet("tensor", ten, T)
    greet("dp", dp, D)
    greeted = 2 * len(tree.near) + T + D - 2
    if tree.far:
        owner_there = lax.rem(seq - tree.far + S, S)

        @pl.when(owner_there + tree.least[tree.far] <= last)
        def _():
            pl.semaphore_signal(barrier, inc=1, device_id={"seq": owner_there}, device_id_type=MESH)

        greeted = greeted + (seq + tree.least[tree.far] <= last).astype(jnp.int32)

    def k_copy(a, b, where):
        return remote(kbuf.at[a], kbuf.at[b], k_send.at[b], k_recv.at[b], {"seq": where})

    def runs(b):
        return lax.rem(seq - b + S, S) + tree.least[b] <= last

    def pass_down(a):
        for b in tree.children[a]:
            @pl.when(lax.rem(seq - a + S, S) + tree.least[b] <= last)
            def _(b=b):
                k_copy(a, b, lax.rem(seq + b - a + S, S)).start()

    def k_arrive(b):
        k_copy(0, b, seq).wait_recv()

    ready("q")
    ready("k")
    ipos = seq * B + lax.broadcasted_iota(jnp.int32, (1, B), 1)
    start = jnp.zeros((1, B), jnp.int32)
    bound = jnp.int32(0)
    for d in range(len_ref.shape[1] - 1):
        bound = bound + len_ref[0, d]
        start = jnp.where(ipos >= bound, bound, start)
    jrow = lax.broadcasted_iota(jnp.int32, (B, B), 0)
    scale = math.log2(math.e) / math.sqrt(HEAD)

    for h in range(2 * pairs):
        qt[h // 2, :, (h % 2) * B : (h % 2 + 1) * B] = qv[:, h * HEAD : (h + 1) * HEAD].T
    m_ref[...] = jnp.full(m_ref.shape, NEG, F32)
    l_ref[...] = jnp.zeros(l_ref.shape, F32)

    def attend(slot):
        jpos = lax.rem(seq - slot + S, S) * B + jrow
        allowed = (jpos >= start) & (jpos <= ipos)
        bias = jnp.where(allowed, 0.0, NEG).astype(F32)
        bias_ref[...] = jnp.concatenate([bias, bias], axis=1)

        for hp in range(pairs):
            x = dot(kbuf[slot, hp // per_kv], qt[hp]) * scale + bias_ref[...]
            old = m_ref[hp]
            new = jnp.maximum(old, jnp.max(x, axis=0, keepdims=True))
            w = jnp.exp2(x - new)
            l_ref[hp] = l_ref[hp] * jnp.exp2(old - new) + jnp.sum(w, axis=0, keepdims=True)
            w_ref[slot, hp] = w.astype(BF16)
            m_ref[hp] = new
            ms_ref[slot, hp] = new

    def attend_on_arrival(slot):
        @pl.when(seq >= slot)
        def _():
            k_arrive(slot)
            attend(slot)

    attend(0)
    pl.semaphore_wait(barrier, greeted)
    pass_down(0)
    for k in range(1, D):
        pl.semaphore_signal(
            met_sem, inc=1, device_id={"dp": lax.rem(dp + k, D)}, device_id_type=MESH
        )

    ready("n")
    xa_buf[0] = dot_general(down[...], nv[...], NT).astype(BF16)

    def xa_copy(k):
        return remote(
            xa_buf.at[0], xa_buf.at[k], xa_send.at[k], xa_recv.at[k], {"tensor": lax.rem(ten + k, T)}
        )

    send([xa_copy(k) for k in range(1, T)], "xa")

    ready("w")

    def dequantised(first, n, put):
        def one(i, carry):
            row = pl.multiple_of(first + i * GROUP, GROUP)
            block = codes[pl.ds(row, GROUP), :].astype(F32)
            put(i, (block * scales[pl.ds(lax.div(row, GROUP), 1), :]).astype(BF16))
            return carry
        lax.fori_loop(0, n // GROUP, one, 0)

    def w_copy(k):
        return remote(
            wst.at[k], wfull.at[k, core], w_send.at[k], w_recv.at[k], {"tensor": lax.rem(ten + k, T)}
        )

    def wc_copy(k, h):
        return remote(wfull.at[k, h], wfull.at[k, h], wc_send.at[k], wc_recv.at[k], {"dp": sibling})

    def send_weights(k):
        def put(i, value):
            wst[k, pl.ds(pl.multiple_of(i * GROUP, GROUP), GROUP), :] = value
        dequantised(lax.rem(ten + k, T) * feats + core * hf, hf, put)
        send([w_copy(k)])

    def own_weights():
        for h in range(2):
            def put(i, value, h=h):
                wfull[0, h, pl.ds(pl.multiple_of(i * GROUP, GROUP), GROUP), :] = value
            dequantised(ten * feats + h * hf, hf, put)


    for n, a in enumerate(tree.relays):
        @pl.when(runs(a))
        def _(a=a):
            k_arrive(a)
            pass_down(a)
        if n + 1 < T:
            send_weights(n + 1)
        for b in tree.after[a]:
            if b in tree.relays:
                @pl.when(seq >= b)
                def _(b=b):
                    attend(b)
            else:
                attend_on_arrival(b)
    for k in range(len(tree.relays) + 1, T):
        send_weights(k)
    coming["w"] = [w_copy(k) for k in range(1, T)]
    for b in tree.final:
        attend_on_arrival(b)

    l_ref[...] = 1.0 / l_ref[...]
    ready("g")

    def partial(slot):
        for g in range(KV):
            total = None
            for i in range(per_kv):
                hp = g * per_kv + i
                factor = jnp.exp2(ms_ref[slot, hp] - m_ref[hp]) * l_ref[hp]
                p = (w_ref[slot, hp].astype(F32) * factor).astype(BF16)
                one = dot(p, gv[hp])
                total = one if total is None else total + one
            acc_ref[g] = total

    def s_copy(a, b, where):
        return remote(rs_out.at[b], rs_in.at[b], s_send.at[b], s_recv.at[b], {"seq": where})

    def up_to(a, b):
        return s_copy(a, b, lax.rem(seq + a - b + S, S))

    def gather(a, keep):
        if a == 0:
            partial(0)
        else:
            @pl.when(seq >= a)
            def _():
                partial(a)

            @pl.when(seq < a)
            def _():
                acc_ref[...] = jnp.zeros(acc_ref.shape, F32)
        for b in tree.children[a]:
            @pl.when(lax.rem(seq - a + S, S) + tree.least[b] <= last)
            def _(b=b):
                s_copy(a, b, seq).wait_recv()
                acc_ref[...] += rs_in[b].astype(F32)
        if keep:
            rs_out[a] = acc_ref[...].astype(BF16)

    for b in tree.up:
        @pl.when(runs(b))
        def _(b=b):
            gather(b, True)
            up_to(tree.parent[b], b).start()

    arrive("xa")
    xat = xa_buf[0].astype(F32)
    for k in range(1, T):
        xat = xat + xa_buf[k].astype(F32)
    xat = xat.astype(BF16)
    arrive("w")
    send([wc_copy(k, core) for k in range(1, T)])
    coming["wc"] = [wc_copy(k, 1 - core) for k in range(1, T)]
    ready("up")
    gather(0, False)
    for g in range(KV):
        dv_buf[0, :, g * HEAD : (g + 1) * HEAD] = acc_ref[g].astype(BF16)

    dv = dv_buf[0]
    gx_buf[0] = dot_general(up[...], dv, NT).astype(BF16)

    def gx_copy(k):
        return remote(
            gx_buf.at[0], gx_buf.at[k], gx_send.at[k], gx_recv.at[k], {"tensor": lax.rem(ten + k, T)}
        )

    def dv_copy(k):
        return remote(
            dv_buf.at[0], dv_buf.at[k], dv_send.at[k], dv_recv.at[k], {"tensor": lax.rem(ten + k, T)}
        )

    send([gx_copy(k) for k in range(1, T)], "gx")
    send([dv_copy(k) for k in range(1, T)], "dv")
    members = D * QUAD
    quads = S // QUAD
    place = lax.rem(seq, QUAD)
    quad = lax.div(seq, QUAD)
    mine = dp * QUAD + place
    wide_a = feats // 128
    wide_b = cols // 128
    n_tiles = (rank // 16) * (wide_a + wide_b)

    def tile_a(i, j):
        n = i * wide_a + j
        return n % members, n // members

    def tile_b(i, j):
        n = (rank // 16) * wide_a + i * wide_b + j
        return n % members, n // members

    per = a_src.shape[1]
    full = n_tiles // members

    def has(piece, slot):
        return slot * members + piece < n_tiles

    part_b = dot(xat, dv)
    for i in range(rank // 16):
        for j in range(cols // 128):
            p, q = tile_b(i, j)
            a_src[p, q] = part_b[i * 16 : i * 16 + 16, j * 128 : j * 128 + 128].astype(BF16)
    arrive("gx")
    gpt = gx_buf[0].astype(F32)
    for k in range(1, T):
        gpt = gpt + gx_buf[k].astype(F32)
    gpt = gpt.astype(BF16)
    for j in range(feats // 128):
        part_a = dot(gpt, nv[:, j * 128 : j * 128 + 128])
        for i in range(rank // 16):
            p, q = tile_a(i, j)
            a_src[p, q] = part_a[i * 16 : i * 16 + 16].astype(BF16)

    def member(k):
        there = lax.rem(dp + lax.div(k, QUAD), D)
        at = lax.rem(place + lax.rem(k, QUAD), QUAD)
        return there * QUAD + at, {"dp": there, "seq": quad * QUAD + at}

    def a_copy(k, slot):
        piece, where = member(k)
        return remote(
            a_src.at[piece, slot], a_rcv.at[k, slot], a_send.at[k, slot], a_recv.at[k, slot], where
        )

    def each(act):
        def one(k, carry):
            act(k)
            return carry
        lax.fori_loop(1, members, one, 0)

    far_first = [
        d * QUAD + z
        for d in sorted(range(D), key=lambda d: -min(d, D - d))
        for z in reversed(range(QUAD))
        if d + z
    ]
    pl.semaphore_wait(met_sem, D - 1)
    for k in far_first:
        for slot in range(full):
            a_copy(k, slot).start()
    for slot in range(full, per):
        @each
        def _(k, slot=slot):
            @pl.when(has(member(k)[0], slot))
            def _():
                a_copy(k, slot).start()
    own_weights()

    def summed(slot):
        def add(k, total):
            a_copy(k, slot).wait_recv()
            return total + a_rcv[k, slot].astype(F32)
        total = lax.fori_loop(1, members, add, a_src[mine, slot].astype(F32))
        b_buf[quad, slot] = total.astype(BF16)

    for slot in range(per):
        if slot < full:
            summed(slot)
        else:
            b_buf[quad, slot] = jnp.zeros((16, 128), BF16)

            @pl.when(has(mine, slot))
            def _(slot=slot):
                summed(slot)

    def b_copy(j):
        there = lax.rem(quad + j, quads)
        return remote(
            b_buf.at[quad], b_buf.at[quad], b_send.at[j], b_recv.at[quad],
            {"seq": there * QUAD + place},
        )

    def b_from(j):
        there = lax.rem(quad + j, quads)
        return remote(
            b_buf.at[there], b_buf.at[there], b_send.at[j], b_recv.at[there],
            {"seq": there * QUAD + place},
        )

    send([b_copy(j) for j in range(1, quads)])
    for j in range(1, quads):
        b_from(j).wait_recv()
    total = b_buf[0].astype(F32)
    for j in range(1, quads):
        total = total + b_buf[j].astype(F32)
    c_buf[...] = total.astype(BF16)

    def d_copy(k, slot):
        where = member(k)[1]
        return remote(
            c_buf.at[slot], d_buf.at[mine, slot], d_send.at[k, slot], d_recv.at[mine, slot], where
        )

    def d_from(k, slot):
        piece, where = member(k)
        return remote(
            c_buf.at[slot], d_buf.at[piece, slot], d_send.at[k, slot], d_recv.at[piece, slot], where
        )

    for k in far_first:
        for slot in range(full):
            d_copy(k, slot).start()
    for slot in range(full, per):
        @pl.when(has(mine, slot))
        def _(slot=slot):
            each(lambda k: d_copy(k, slot).start())
    d_buf[mine] = c_buf[...]

    gp = gpt.T
    arrive("dv")
    arrive("wc")
    width = min(256, hf)
    for n in range(feats // width):
        h, row = n * width // hf, n * width % hf
        at = slice(n * width, (n + 1) * width)
        total = 2.0 * dot(gp, down[:, at])
        for k in range(T):
            total = total + dot_general(dv_buf[k], wfull[k, h, row : row + width, :], NT)
        dn_ref[:, at] = total.astype(BF16)

    for slot in range(per):
        @each
        def _(k, slot=slot):
            @pl.when(has(member(k)[0], slot))
            def _():
                d_from(k, slot).wait_recv()
    factor = 2.0 / math.sqrt(D * S * B)
    for i in range(rank // 16):
        at = slice(i * 16, i * 16 + 16)
        for j in range(wide_a):
            ga_ref[at, j * 128 : j * 128 + 128] = d_buf[tile_a(i, j)].astype(F32) * factor
        for j in range(wide_b):
            gb_ref[at, j * 128 : j * 128 + 128] = d_buf[tile_b(i, j)].astype(F32) * factor

    for c in sent:
        c.wait_send()
    for b, a in tree.parent.items():

        @pl.when(lax.rem(seq - a + S, S) + tree.least[b] <= last)
        def _(a=a, b=b):
            k_copy(a, b, seq).wait_send()

        @pl.when(runs(b))
        def _(b=b):
            up_to(a, b).wait_send()
    for slot in range(per):
        @each
        def _(k, slot=slot):
            @pl.when(has(member(k)[0], slot))
            def _():
                a_copy(k, slot).wait_send()

            @pl.when(has(mine, slot))
            def _():
                d_copy(k, slot).wait_send()


def body(
    shape, queries, keys, output_gradient, normed, document_length, codes, scales,
    adapter_down, adapter_up,
):
    D, S, T = shape
    B = queries.shape[1]
    heads = queries.shape[2] // HEAD
    pairs = heads // 2
    feats = normed.shape[2]
    rank, cols = adapter_up.shape
    members = D * QUAD
    per = -(-(rank // 16) * ((feats + cols) // 128) // members)
    hbm = pl.BlockSpec(memory_space=pltpu.HBM)
    vmem = pl.BlockSpec(memory_space=pltpu.VMEM)
    dma = pltpu.SemaphoreType.DMA
    d_normed, grad_a, grad_b = pl.pallas_call(
        functools.partial(kernel, shape),
        out_shape=(
            jax.ShapeDtypeStruct((B, feats), BF16),
            jax.ShapeDtypeStruct((rank, feats), F32),
            jax.ShapeDtypeStruct((rank, cols), F32),
        ),
        in_specs=[hbm] * 9,
        out_specs=(vmem, vmem, vmem),
        scratch_shapes=[
            pltpu.SMEM(document_length.shape, jnp.int32),
            pltpu.VMEM((S, KV, B, HEAD), BF16),
            pltpu.VMEM((B, heads * HEAD), BF16),
            pltpu.VMEM((pairs, HEAD, 2 * B), BF16),
            pltpu.VMEM((pairs, 2 * B, HEAD), BF16),
            pltpu.VMEM((B, feats), BF16),
            pltpu.VMEM(codes.shape, BF16),
            pltpu.VMEM(scales.shape, F32),
            pltpu.VMEM((rank, feats), BF16),
            pltpu.VMEM((rank, cols), BF16),
            pltpu.VMEM((T, feats // 2, cols), BF16),
            pltpu.VMEM((T, 2, feats // 2, cols), BF16),
            pltpu.VMEM((B, 2 * B), F32),
            pltpu.VMEM((pairs, 1, 2 * B), F32),
            pltpu.VMEM((pairs, 1, 2 * B), F32),
            pltpu.VMEM((S, pairs, 1, 2 * B), F32),
            pltpu.VMEM((S, pairs, B, 2 * B), BF16),
            pltpu.VMEM((KV, B, HEAD), F32),
            pltpu.VMEM((S, KV, B, HEAD), BF16),
            pltpu.VMEM((S, KV, B, HEAD), BF16),
            pltpu.VMEM((T, rank, B), BF16),
            pltpu.VMEM((T, rank, B), BF16),
            pltpu.VMEM((T, B, cols), BF16),
            pltpu.VMEM((members, per, 16, 128), BF16),
            pltpu.VMEM((members, per, 16, 128), BF16),
            pltpu.VMEM((S // QUAD, per, 16, 128), BF16),
            pltpu.VMEM((per, 16, 128), BF16),
            pltpu.VMEM((members, per, 16, 128), BF16),
            pltpu.SemaphoreType.REGULAR,
            dma((9 + heads,)),
            dma((S,)),
            dma((S,)),
            dma((S,)),
            dma((S,)),
            dma((T,)),
            dma((T,)),
            dma((T,)),
            dma((T,)),
            dma((T,)),
            dma((T,)),
            dma((T,)),
            dma((T,)),
            dma((T,)),
            dma((T,)),
            dma((members, per)),
            dma((members, per)),
            dma((S // QUAD,)),
            dma((S // QUAD,)),
            dma((members, per)),
            dma((members, per)),
        ],
        compiler_params=pltpu.CompilerParams(
            collective_id=0, has_side_effects=True, vmem_limit_bytes=40 * 1024 * 1024
        ),
        name="value_backward",
    )(
        *(
            pltpu.with_memory_space_constraint(x, pltpu.HBM)
            for x in (
                queries[0], keys[0], output_gradient[0], normed[0], document_length, codes,
                scales, adapter_down.T, adapter_up,
            )
        )
    )
    return d_normed[None], grad_a.T, grad_b


def solution(mesh):
    shape = tuple(mesh.shape[a] for a in ("dp", "seq", "tensor"))
    split = P("dp", "seq", "tensor")
    placed = (
        split, split, split, split,
        P("dp", None), P(None, "tensor"), P(None, "tensor"), P("tensor", None), P(None, "tensor"),
    )
    return jax.shard_map(
        functools.partial(body, shape),
        mesh=mesh,
        in_specs=placed,
        out_specs=(split, P("tensor", None), P(None, "tensor")),
        check_vma=False,
    )
```

```python
import functools
import math

import jax
import jax.numpy as jnp
from jax import lax
from jax.experimental import pallas as pl
from jax.experimental.pallas import tpu as pltpu
from jax.sharding import PartitionSpec as P

MESH = pl.DeviceIdType.MESH
HEAD = 128
GROUP = 128
KV = 2
QUAD = 4
NEG = -1e30
F32 = jnp.float32
BF16 = jnp.bfloat16
NT = (((1,), (1,)), ((), ()))
TN = (((0,), (0,)), ((), ()))


def dot(a, b):
    return jnp.dot(a, b, preferred_element_type=F32)


def dot_general(a, b, dims):
    return lax.dot_general(a, b, dims, preferred_element_type=F32)


class Tree:
    def __init__(self, size):
        if size == 16:
            self.parent = {3: 0, 1: 0, 11: 0, 6: 3, 2: 3, 12: 11, 10: 11, 9: 11}
            self.parent.update({8: 6, 4: 6, 7: 6, 5: 6})
            self.after = {3: [], 11: [3, 1, 11], 6: [2, 6]}
            self.final = [12, 10, 9, 7, 5, 8, 4]
            self.up = [8, 4, 7, 5, 12, 10, 9, 2, 1, 6, 11, 3]
            self.far = 11
        else:
            self.parent = {b: b - 1 for b in range(1, size)}
            self.after = {b: [b] for b in range(1, size - 1)}
            self.final = [size - 1]
            self.up = list(range(size - 1, 0, -1))
            self.far = None
        self.near = [k for k in (1, 2, 3) if 2 * k <= size]
        self.relays = list(self.after)
        self.children = {a: [b for b in self.parent if self.parent[b] == a] for a in range(size)}
        self.least = {b: min(self.below(b)) for b in self.parent}

    def below(self, b):
        return [b] + [x for child in self.children[b] for x in self.below(child)]


def kernel(
    shape,
    q_hbm, k_hbm, g_hbm, n_hbm, len_hbm, codes_hbm, scales_hbm, down_hbm, up_hbm,
    dn_ref, ga_ref, gb_ref,
    len_ref, kbuf, qv, qt, gv, nv, codes, scales, down, up, wst, wfull, bias_ref,
    m_ref, l_ref, ms_ref, w_ref, acc_ref, rs_out, rs_in, xa_buf, gx_buf, dv_buf,
    a_src, a_rcv, b_buf, c_buf, d_buf,
    met_sem, local_sem, k_send, k_recv, s_send, s_recv,
    w_send, w_recv, wc_send, wc_recv, xa_send, xa_recv, gx_send, gx_recv,
    dv_send, dv_recv, a_send, a_recv, b_send, b_recv, d_send, d_recv,
):
    D, S, T = shape
    tree = Tree(S)
    B = kbuf.shape[2]
    pairs = qt.shape[0]
    per_kv = pairs // KV
    feats = nv.shape[1]
    rank = up.shape[0]
    cols = up.shape[1]
    hf = feats // 2
    dp = lax.axis_index("dp")
    seq = lax.axis_index("seq")
    ten = lax.axis_index("tensor")
    core = lax.rem(dp, 2)
    sibling = dp + 1 - 2 * core
    last = S - 1

    def remote(src, dst, send, recv, where):
        return pltpu.make_async_remote_copy(
            src_ref=src, dst_ref=dst, send_sem=send, recv_sem=recv,
            device_id=where, device_id_type=MESH,
        )

    def local(src, dst, i):
        return pltpu.make_async_copy(src, dst, local_sem.at[i])

    in_k = [local(k_hbm.at[:, pl.ds(g * HEAD, HEAD)], kbuf.at[0, g], g) for g in range(KV)]
    in_q = local(q_hbm, qv, 2)
    in_codes = local(codes_hbm, codes, 3)
    in_scales = local(scales_hbm, scales, 4)
    in_n = local(n_hbm, nv, 5)
    in_down = local(down_hbm, down, 6)
    in_up = local(up_hbm, up, 7)
    in_len = local(len_hbm, len_ref, 8)
    in_g = [
        local(
            g_hbm.at[:, pl.ds(h * HEAD, HEAD)],
            gv.at[h // 2, pl.ds((h % 2) * B, B), :],
            9 + h,
        )
        for h in range(2 * pairs)
    ]
    due = {"k": in_k, "q": [in_q, in_len], "n": [in_n, in_down], "w": [in_codes, in_scales]}
    due.update({"g": in_g, "up": [in_up]})
    for group in ("k", "q", "n", "w", "g", "up"):
        for c in due[group]:
            c.start()

    def ready(group):
        for c in due.pop(group):
            c.wait()

    sent = []
    coming = {}

    def send(copies, group=None):
        for c in copies:
            c.start()
        sent.extend(copies)
        if group:
            coming[group] = copies

    def arrive(group):
        for c in coming.pop(group):
            c.wait_recv()

    barrier = pltpu.get_barrier_semaphore()

    def greet(axis, me, size):
        def one(k, carry):
            pl.semaphore_signal(
                barrier, inc=1, device_id={axis: lax.rem(me + k, size)}, device_id_type=MESH
            )
            return carry
        lax.fori_loop(1, size, one, 0)

    for k in tree.near:
        for away in (k, S - k):
            pl.semaphore_signal(
                barrier, inc=1, device_id={"seq": lax.rem(seq + away, S)}, device_id_type=MESH
            )
    greet("tensor", ten, T)
    greet("dp", dp, D)
    greeted = 2 * len(tree.near) + T + D - 2
    if tree.far:
        owner_there = lax.rem(seq - tree.far + S, S)

        @pl.when(owner_there + tree.least[tree.far] <= last)
        def _():
            pl.semaphore_signal(barrier, inc=1, device_id={"seq": owner_there}, device_id_type=MESH)

        greeted = greeted + (seq + tree.least[tree.far] <= last).astype(jnp.int32)

    def k_copy(a, b, g, where):
        return remote(
            kbuf.at[a, g], kbuf.at[b, g], k_send.at[b, g], k_recv.at[b, g], {"seq": where}
        )

    def runs(b):
        return lax.rem(seq - b + S, S) + tree.least[b] <= last

    def pass_down(a, g):
        for b in tree.children[a]:
            @pl.when(lax.rem(seq - a + S, S) + tree.least[b] <= last)
            def _(b=b):
                k_copy(a, b, g, lax.rem(seq + b - a + S, S)).start()

    def k_arrive(b):
        for g in range(KV):
            k_copy(0, b, g, seq).wait_recv()

    ready("q")
    ready("k")
    ipos = seq * B + lax.broadcasted_iota(jnp.int32, (1, B), 1)
    start = jnp.zeros((1, B), jnp.int32)
    bound = jnp.int32(0)
    for d in range(len_ref.shape[1] - 1):
        bound = bound + len_ref[0, d]
        start = jnp.where(ipos >= bound, bound, start)
    jrow = lax.broadcasted_iota(jnp.int32, (B, B), 0)
    scale = math.log2(math.e) / math.sqrt(HEAD)

    for h in range(2 * pairs):
        qt[h // 2, :, (h % 2) * B : (h % 2 + 1) * B] = qv[:, h * HEAD : (h + 1) * HEAD].T
    m_ref[...] = jnp.full(m_ref.shape, NEG, F32)
    l_ref[...] = jnp.zeros(l_ref.shape, F32)

    def attend(slot):
        jpos = lax.rem(seq - slot + S, S) * B + jrow
        allowed = (jpos >= start) & (jpos <= ipos)
        bias = jnp.where(allowed, 0.0, NEG).astype(F32)
        bias_ref[...] = jnp.concatenate([bias, bias], axis=1)

        for hp in range(pairs):
            x = dot(kbuf[slot, hp // per_kv], qt[hp]) * scale + bias_ref[...]
            old = m_ref[hp]
            new = jnp.maximum(old, jnp.max(x, axis=0, keepdims=True))
            w = jnp.exp2(x - new)
            l_ref[hp] = l_ref[hp] * jnp.exp2(old - new) + jnp.sum(w, axis=0, keepdims=True)
            w_ref[slot, hp] = w.astype(BF16)
            m_ref[hp] = new
            ms_ref[slot, hp] = new

    def attend_on_arrival(slot):
        @pl.when(seq >= slot)
        def _():
            k_arrive(slot)
            attend(slot)

    attend(0)
    pl.semaphore_wait(barrier, greeted)
    for g in range(KV):
        pass_down(0, g)
    for k in range(1, D):
        pl.semaphore_signal(
            met_sem, inc=1, device_id={"dp": lax.rem(dp + k, D)}, device_id_type=MESH
        )

    ready("n")
    xa_buf[0] = dot_general(down[...], nv[...], NT).astype(BF16)

    def xa_copy(k):
        return remote(
            xa_buf.at[0], xa_buf.at[k], xa_send.at[k], xa_recv.at[k], {"tensor": lax.rem(ten + k, T)}
        )

    send([xa_copy(k) for k in range(1, T)], "xa")

    ready("w")

    def dequantised(first, n, put):
        def one(i, carry):
            row = pl.multiple_of(first + i * GROUP, GROUP)
            block = codes[pl.ds(row, GROUP), :].astype(F32)
            put(i, (block * scales[pl.ds(lax.div(row, GROUP), 1), :]).astype(BF16))
            return carry
        lax.fori_loop(0, n // GROUP, one, 0)

    def w_copy(k):
        return remote(
            wst.at[k], wfull.at[k, core], w_send.at[k], w_recv.at[k], {"tensor": lax.rem(ten + k, T)}
        )

    def wc_copy(k, h):
        return remote(wfull.at[k, h], wfull.at[k, h], wc_send.at[k], wc_recv.at[k], {"dp": sibling})

    def send_weights(k):
        def put(i, value):
            wst[k, pl.ds(pl.multiple_of(i * GROUP, GROUP), GROUP), :] = value
        dequantised(lax.rem(ten + k, T) * feats + core * hf, hf, put)
        send([w_copy(k)])

    def own_weights():
        for h in range(2):
            def put(i, value, h=h):
                wfull[0, h, pl.ds(pl.multiple_of(i * GROUP, GROUP), GROUP), :] = value
            dequantised(ten * feats + h * hf, hf, put)


    for n, a in enumerate(tree.relays):
        @pl.when(runs(a))
        def _(a=a):
            for g in range(KV):
                k_copy(0, a, g, seq).wait_recv()
                pass_down(a, g)
        if n + 1 < T:
            send_weights(n + 1)
        for b in tree.after[a]:
            if b in tree.relays:
                @pl.when(seq >= b)
                def _(b=b):
                    attend(b)
            else:
                attend_on_arrival(b)
    for k in range(len(tree.relays) + 1, T):
        send_weights(k)
    coming["w"] = [w_copy(k) for k in range(1, T)]
    for b in tree.final:
        attend_on_arrival(b)

    l_ref[...] = 1.0 / l_ref[...]
    ready("g")

    def partial(slot, g):
        total = None
        for i in range(per_kv):
            hp = g * per_kv + i
            factor = jnp.exp2(ms_ref[slot, hp] - m_ref[hp]) * l_ref[hp]
            p = (w_ref[slot, hp].astype(F32) * factor).astype(BF16)
            one = dot(p, gv[hp])
            total = one if total is None else total + one
        acc_ref[g] = total

    def s_copy(b, g, where):
        return remote(
            rs_out.at[b, g], rs_in.at[b, g], s_send.at[b, g], s_recv.at[b, g], {"seq": where}
        )

    def up_from(b, g):
        return s_copy(b, g, lax.rem(seq + tree.parent[b] - b + S, S))

    def gather(a, g):
        if a == 0:
            partial(0, g)
        else:
            @pl.when(seq >= a)
            def _():
                partial(a, g)

            @pl.when(seq < a)
            def _():
                acc_ref[g] = jnp.zeros((B, HEAD), F32)
        for b in tree.children[a]:
            @pl.when(lax.rem(seq - a + S, S) + tree.least[b] <= last)
            def _(b=b):
                s_copy(b, g, seq).wait_recv()
                acc_ref[g] += rs_in[b, g].astype(F32)

    for b in tree.up:
        @pl.when(runs(b))
        def _(b=b):
            for g in range(KV):
                gather(b, g)
                rs_out[b, g] = acc_ref[g].astype(BF16)
                up_from(b, g).start()

    arrive("xa")
    xat = xa_buf[0].astype(F32)
    for k in range(1, T):
        xat = xat + xa_buf[k].astype(F32)
    xat = xat.astype(BF16)
    arrive("w")
    send([wc_copy(k, core) for k in range(1, T)])
    coming["wc"] = [wc_copy(k, 1 - core) for k in range(1, T)]
    ready("up")
    for g in range(KV):
        gather(0, g)
        dv_buf[0, :, g * HEAD : (g + 1) * HEAD] = acc_ref[g].astype(BF16)

    dv = dv_buf[0]
    gx_buf[0] = dot_general(up[...], dv, NT).astype(BF16)

    def gx_copy(k):
        return remote(
            gx_buf.at[0], gx_buf.at[k], gx_send.at[k], gx_recv.at[k], {"tensor": lax.rem(ten + k, T)}
        )

    def dv_copy(k):
        return remote(
            dv_buf.at[0], dv_buf.at[k], dv_send.at[k], dv_recv.at[k], {"tensor": lax.rem(ten + k, T)}
        )

    send([gx_copy(k) for k in range(1, T)], "gx")
    send([dv_copy(k) for k in range(1, T)], "dv")
    members = D * QUAD
    quads = S // QUAD
    place = lax.rem(seq, QUAD)
    quad = lax.div(seq, QUAD)
    mine = dp * QUAD + place
    wide_a = feats // 128
    wide_b = cols // 128
    n_tiles = (rank // 16) * (wide_a + wide_b)

    def tile_a(i, j):
        n = i * wide_a + j
        return n % members, n // members

    def tile_b(i, j):
        n = (rank // 16) * wide_a + i * wide_b + j
        return n % members, n // members

    per = a_src.shape[1]
    full = n_tiles // members

    def has(piece, slot):
        return slot * members + piece < n_tiles

    part_b = dot(xat, dv)
    for i in range(rank // 16):
        for j in range(cols // 128):
            p, q = tile_b(i, j)
            a_src[p, q] = part_b[i * 16 : i * 16 + 16, j * 128 : j * 128 + 128].astype(BF16)
    arrive("gx")
    gpt = gx_buf[0].astype(F32)
    for k in range(1, T):
        gpt = gpt + gx_buf[k].astype(F32)
    gpt = gpt.astype(BF16)
    for j in range(feats // 128):
        part_a = dot(gpt, nv[:, j * 128 : j * 128 + 128])
        for i in range(rank // 16):
            p, q = tile_a(i, j)
            a_src[p, q] = part_a[i * 16 : i * 16 + 16].astype(BF16)

    def member(k):
        there = lax.rem(dp + lax.div(k, QUAD), D)
        at = lax.rem(place + lax.rem(k, QUAD), QUAD)
        return there * QUAD + at, {"dp": there, "seq": quad * QUAD + at}

    def a_copy(k, slot):
        piece, where = member(k)
        return remote(
            a_src.at[piece, slot], a_rcv.at[k, slot], a_send.at[k, slot], a_recv.at[k, slot], where
        )

    def each(act):
        def one(k, carry):
            act(k)
            return carry
        lax.fori_loop(1, members, one, 0)

    far_first = [
        d * QUAD + z
        for d in sorted(range(D), key=lambda d: -min(d, D - d))
        for z in reversed(range(QUAD))
        if d + z
    ]
    pl.semaphore_wait(met_sem, D - 1)
    for k in far_first:
        for slot in range(full):
            a_copy(k, slot).start()
    for slot in range(full, per):
        @each
        def _(k, slot=slot):
            @pl.when(has(member(k)[0], slot))
            def _():
                a_copy(k, slot).start()
    own_weights()

    def summed(slot):
        def add(k, total):
            a_copy(k, slot).wait_recv()
            return total + a_rcv[k, slot].astype(F32)
        total = lax.fori_loop(1, members, add, a_src[mine, slot].astype(F32))
        b_buf[quad, slot] = total.astype(BF16)

    for slot in range(per):
        if slot < full:
            summed(slot)
        else:
            b_buf[quad, slot] = jnp.zeros((16, 128), BF16)

            @pl.when(has(mine, slot))
            def _(slot=slot):
                summed(slot)

    def b_copy(j):
        there = lax.rem(quad + j, quads)
        return remote(
            b_buf.at[quad], b_buf.at[quad], b_send.at[j], b_recv.at[quad],
            {"seq": there * QUAD + place},
        )

    def b_from(j):
        there = lax.rem(quad + j, quads)
        return remote(
            b_buf.at[there], b_buf.at[there], b_send.at[j], b_recv.at[there],
            {"seq": there * QUAD + place},
        )

    send([b_copy(j) for j in range(1, quads)])

    gp = gpt.T
    arrive("dv")
    arrive("wc")
    width = min(256, hf)
    for n in range(feats // width):
        h, row = n * width // hf, n * width % hf
        at = slice(n * width, (n + 1) * width)
        total = 2.0 * dot(gp, down[:, at])
        for k in range(T):
            total = total + dot_general(dv_buf[k], wfull[k, h, row : row + width, :], NT)
        dn_ref[:, at] = total.astype(BF16)


    for j in range(1, quads):
        b_from(j).wait_recv()
    sums = b_buf[0].astype(F32)
    for j in range(1, quads):
        sums = sums + b_buf[j].astype(F32)
    c_buf[...] = sums.astype(BF16)

    def d_copy(k, slot):
        where = member(k)[1]
        return remote(
            c_buf.at[slot], d_buf.at[mine, slot], d_send.at[k, slot], d_recv.at[mine, slot], where
        )

    def d_from(k, slot):
        piece, where = member(k)
        return remote(
            c_buf.at[slot], d_buf.at[piece, slot], d_send.at[k, slot], d_recv.at[piece, slot], where
        )

    for k in far_first:
        for slot in range(full):
            d_copy(k, slot).start()
    for slot in range(full, per):
        @pl.when(has(mine, slot))
        def _(slot=slot):
            each(lambda k: d_copy(k, slot).start())
    d_buf[mine] = c_buf[...]

    for slot in range(per):
        @each
        def _(k, slot=slot):
            @pl.when(has(member(k)[0], slot))
            def _():
                d_from(k, slot).wait_recv()
    factor = 2.0 / math.sqrt(D * S * B)
    for i in range(rank // 16):
        at = slice(i * 16, i * 16 + 16)
        for j in range(wide_a):
            ga_ref[at, j * 128 : j * 128 + 128] = d_buf[tile_a(i, j)].astype(F32) * factor
        for j in range(wide_b):
            gb_ref[at, j * 128 : j * 128 + 128] = d_buf[tile_b(i, j)].astype(F32) * factor

    for c in sent:
        c.wait_send()
    for b, a in tree.parent.items():

        @pl.when(lax.rem(seq - a + S, S) + tree.least[b] <= last)
        def _(a=a, b=b):
            for g in range(KV):
                k_copy(a, b, g, seq).wait_send()

        @pl.when(runs(b))
        def _(b=b):
            for g in range(KV):
                up_from(b, g).wait_send()
    for slot in range(per):
        @each
        def _(k, slot=slot):
            @pl.when(has(member(k)[0], slot))
            def _():
                a_copy(k, slot).wait_send()

            @pl.when(has(mine, slot))
            def _():
                d_copy(k, slot).wait_send()


def body(
    shape, queries, keys, output_gradient, normed, document_length, codes, scales,
    adapter_down, adapter_up,
):
    D, S, T = shape
    B = queries.shape[1]
    heads = queries.shape[2] // HEAD
    pairs = heads // 2
    feats = normed.shape[2]
    rank, cols = adapter_up.shape
    members = D * QUAD
    per = -(-(rank // 16) * ((feats + cols) // 128) // members)
    hbm = pl.BlockSpec(memory_space=pltpu.HBM)
    vmem = pl.BlockSpec(memory_space=pltpu.VMEM)
    dma = pltpu.SemaphoreType.DMA
    d_normed, grad_a, grad_b = pl.pallas_call(
        functools.partial(kernel, shape),
        out_shape=(
            jax.ShapeDtypeStruct((B, feats), BF16),
            jax.ShapeDtypeStruct((rank, feats), F32),
            jax.ShapeDtypeStruct((rank, cols), F32),
        ),
        in_specs=[hbm] * 9,
        out_specs=(vmem, vmem, vmem),
        scratch_shapes=[
            pltpu.SMEM(document_length.shape, jnp.int32),
            pltpu.VMEM((S, KV, B, HEAD), BF16),
            pltpu.VMEM((B, heads * HEAD), BF16),
            pltpu.VMEM((pairs, HEAD, 2 * B), BF16),
            pltpu.VMEM((pairs, 2 * B, HEAD), BF16),
            pltpu.VMEM((B, feats), BF16),
            pltpu.VMEM(codes.shape, BF16),
            pltpu.VMEM(scales.shape, F32),
            pltpu.VMEM((rank, feats), BF16),
            pltpu.VMEM((rank, cols), BF16),
            pltpu.VMEM((T, feats // 2, cols), BF16),
            pltpu.VMEM((T, 2, feats // 2, cols), BF16),
            pltpu.VMEM((B, 2 * B), F32),
            pltpu.VMEM((pairs, 1, 2 * B), F32),
            pltpu.VMEM((pairs, 1, 2 * B), F32),
            pltpu.VMEM((S, pairs, 1, 2 * B), F32),
            pltpu.VMEM((S, pairs, B, 2 * B), BF16),
            pltpu.VMEM((KV, B, HEAD), F32),
            pltpu.VMEM((S, KV, B, HEAD), BF16),
            pltpu.VMEM((S, KV, B, HEAD), BF16),
            pltpu.VMEM((T, rank, B), BF16),
            pltpu.VMEM((T, rank, B), BF16),
            pltpu.VMEM((T, B, cols), BF16),
            pltpu.VMEM((members, per, 16, 128), BF16),
            pltpu.VMEM((members, per, 16, 128), BF16),
            pltpu.VMEM((S // QUAD, per, 16, 128), BF16),
            pltpu.VMEM((per, 16, 128), BF16),
            pltpu.VMEM((members, per, 16, 128), BF16),
            pltpu.SemaphoreType.REGULAR,
            dma((9 + heads,)),
            dma((S, KV)),
            dma((S, KV)),
            dma((S, KV)),
            dma((S, KV)),
            dma((T,)),
            dma((T,)),
            dma((T,)),
            dma((T,)),
            dma((T,)),
            dma((T,)),
            dma((T,)),
            dma((T,)),
            dma((T,)),
            dma((T,)),
            dma((members, per)),
            dma((members, per)),
            dma((S // QUAD,)),
            dma((S // QUAD,)),
            dma((members, per)),
            dma((members, per)),
        ],
        compiler_params=pltpu.CompilerParams(
            collective_id=0, has_side_effects=True, vmem_limit_bytes=40 * 1024 * 1024
        ),
        name="value_backward",
    )(
        *(
            pltpu.with_memory_space_constraint(x, pltpu.HBM)
            for x in (
                queries[0], keys[0], output_gradient[0], normed[0], document_length, codes,
                scales, adapter_down.T, adapter_up,
            )
        )
    )
    return d_normed[None], grad_a.T, grad_b


def solution(mesh):
    shape = tuple(mesh.shape[a] for a in ("dp", "seq", "tensor"))
    split = P("dp", "seq", "tensor")
    placed = (
        split, split, split, split,
        P("dp", None), P(None, "tensor"), P(None, "tensor"), P("tensor", None), P(None, "tensor"),
    )
    return jax.shard_map(
        functools.partial(body, shape),
        mesh=mesh,
        in_specs=placed,
        out_specs=(split, P("tensor", None), P(None, "tensor")),
        check_vma=False,
    )
```

```python
import functools
import math

import jax
import jax.numpy as jnp
from jax import lax
from jax.experimental import pallas as pl
from jax.experimental.pallas import tpu as pltpu
from jax.sharding import PartitionSpec as P

MESH = pl.DeviceIdType.MESH
HEAD = 128
GROUP = 128
KV = 2
QUAD = 4
NEG = -1e30
F32 = jnp.float32
BF16 = jnp.bfloat16
NT = (((1,), (1,)), ((), ()))
TN = (((0,), (0,)), ((), ()))


def dot(a, b):
    return jnp.dot(a, b, preferred_element_type=F32)


def dot_general(a, b, dims):
    return lax.dot_general(a, b, dims, preferred_element_type=F32)


class Tree:
    def __init__(self, size):
        if size == 16:
            self.parent = {3: 0, 1: 0, 11: 0, 6: 3, 2: 3, 12: 11, 10: 11, 9: 11}
            self.parent.update({4: 3, 8: 6, 7: 6, 5: 6})
            self.after = {3: [], 11: [3, 1, 11], 6: [2, 6]}
            self.final = [4, 12, 10, 9, 7, 5, 8]
            self.up = [8, 7, 5, 4, 12, 10, 9, 2, 1, 6, 11, 3]
            self.far = 11
        else:
            self.parent = {b: b - 1 for b in range(1, size)}
            self.after = {b: [b] for b in range(1, size - 1)}
            self.final = [size - 1]
            self.up = list(range(size - 1, 0, -1))
            self.far = None
        self.near = [k for k in (1, 2, 3) if 2 * k <= size]
        self.relays = list(self.after)
        self.children = {a: [b for b in self.parent if self.parent[b] == a] for a in range(size)}
        self.least = {b: min(self.below(b)) for b in self.parent}

    def below(self, b):
        return [b] + [x for child in self.children[b] for x in self.below(child)]


def kernel(
    shape,
    q_hbm, k_hbm, g_hbm, n_hbm, len_hbm, codes_hbm, scales_hbm, down_hbm, up_hbm,
    dn_ref, ga_ref, gb_ref,
    len_ref, kbuf, qv, qt, gv, nv, codes, scales, down, up, wst, wfull, bias_ref,
    m_ref, l_ref, ms_ref, w_ref, acc_ref, rs_out, rs_in, xa_buf, gx_buf, dv_buf,
    a_src, a_rcv, b_buf, c_buf, d_buf,
    met_sem, local_sem, k_send, k_recv, s_send, s_recv,
    w_send, w_recv, wc_send, wc_recv, xa_send, xa_recv, gx_send, gx_recv,
    dv_send, dv_recv, a_send, a_recv, b_send, b_recv, d_send, d_recv,
):
    D, S, T = shape
    tree = Tree(S)
    B = kbuf.shape[2]
    pairs = qt.shape[0]
    per_kv = pairs // KV
    feats = nv.shape[1]
    rank = up.shape[0]
    cols = up.shape[1]
    hf = feats // 2
    dp = lax.axis_index("dp")
    seq = lax.axis_index("seq")
    ten = lax.axis_index("tensor")
    core = lax.rem(dp, 2)
    sibling = dp + 1 - 2 * core
    last = S - 1

    def remote(src, dst, send, recv, where):
        return pltpu.make_async_remote_copy(
            src_ref=src, dst_ref=dst, send_sem=send, recv_sem=recv,
            device_id=where, device_id_type=MESH,
        )

    def local(src, dst, i):
        return pltpu.make_async_copy(src, dst, local_sem.at[i])

    in_k = [local(k_hbm.at[:, pl.ds(g * HEAD, HEAD)], kbuf.at[0, g], g) for g in range(KV)]
    in_q = local(q_hbm, qv, 2)
    in_codes = local(codes_hbm, codes, 3)
    in_scales = local(scales_hbm, scales, 4)
    in_n = local(n_hbm, nv, 5)
    in_down = local(down_hbm, down, 6)
    in_up = local(up_hbm, up, 7)
    in_len = local(len_hbm, len_ref, 8)
    in_g = [
        local(
            g_hbm.at[:, pl.ds(h * HEAD, HEAD)],
            gv.at[h // 2, pl.ds((h % 2) * B, B), :],
            9 + h,
        )
        for h in range(2 * pairs)
    ]
    due = {"k": in_k, "q": [in_q, in_len], "n": [in_n, in_down], "w": [in_codes, in_scales]}
    due.update({"g": in_g, "up": [in_up]})
    for group in ("k", "q", "n", "w", "g", "up"):
        for c in due[group]:
            c.start()

    def ready(group):
        for c in due.pop(group):
            c.wait()

    sent = []
    coming = {}

    def send(copies, group=None):
        for c in copies:
            c.start()
        sent.extend(copies)
        if group:
            coming[group] = copies

    def arrive(group):
        for c in coming.pop(group):
            c.wait_recv()

    barrier = pltpu.get_barrier_semaphore()

    def greet(axis, me, size):
        def one(k, carry):
            pl.semaphore_signal(
                barrier, inc=1, device_id={axis: lax.rem(me + k, size)}, device_id_type=MESH
            )
            return carry
        lax.fori_loop(1, size, one, 0)

    for k in tree.near:
        for away in (k, S - k):
            pl.semaphore_signal(
                barrier, inc=1, device_id={"seq": lax.rem(seq + away, S)}, device_id_type=MESH
            )
    greet("tensor", ten, T)
    greet("dp", dp, D)
    greeted = 2 * len(tree.near) + T + D - 2
    if tree.far:
        owner_there = lax.rem(seq - tree.far + S, S)

        @pl.when(owner_there + tree.least[tree.far] <= last)
        def _():
            pl.semaphore_signal(barrier, inc=1, device_id={"seq": owner_there}, device_id_type=MESH)

        greeted = greeted + (seq + tree.least[tree.far] <= last).astype(jnp.int32)

    def k_copy(a, b, where):
        return remote(kbuf.at[a], kbuf.at[b], k_send.at[b], k_recv.at[b], {"seq": where})

    def runs(b):
        return lax.rem(seq - b + S, S) + tree.least[b] <= last

    def pass_down(a):
        for b in tree.children[a]:
            @pl.when(lax.rem(seq - a + S, S) + tree.least[b] <= last)
            def _(b=b):
                k_copy(a, b, lax.rem(seq + b - a + S, S)).start()

    def k_arrive(b):
        k_copy(0, b, seq).wait_recv()

    ready("q")
    ready("k")
    ipos = seq * B + lax.broadcasted_iota(jnp.int32, (1, B), 1)
    start = jnp.zeros((1, B), jnp.int32)
    bound = jnp.int32(0)
    for d in range(len_ref.shape[1] - 1):
        bound = bound + len_ref[0, d]
        start = jnp.where(ipos >= bound, bound, start)
    jrow = lax.broadcasted_iota(jnp.int32, (B, B), 0)
    scale = math.log2(math.e) / math.sqrt(HEAD)

    for h in range(2 * pairs):
        qt[h // 2, :, (h % 2) * B : (h % 2 + 1) * B] = qv[:, h * HEAD : (h + 1) * HEAD].T
    m_ref[...] = jnp.full(m_ref.shape, NEG, F32)
    l_ref[...] = jnp.zeros(l_ref.shape, F32)

    def attend(slot):
        jpos = lax.rem(seq - slot + S, S) * B + jrow
        allowed = (jpos >= start) & (jpos <= ipos)
        bias = jnp.where(allowed, 0.0, NEG).astype(F32)
        bias_ref[...] = jnp.concatenate([bias, bias], axis=1)

        for hp in range(pairs):
            x = dot(kbuf[slot, hp // per_kv], qt[hp]) * scale + bias_ref[...]
            old = m_ref[hp]
            new = jnp.maximum(old, jnp.max(x, axis=0, keepdims=True))
            w = jnp.exp2(x - new)
            l_ref[hp] = l_ref[hp] * jnp.exp2(old - new) + jnp.sum(w, axis=0, keepdims=True)
            w_ref[slot, hp] = w.astype(BF16)
            m_ref[hp] = new
            ms_ref[slot, hp] = new

    def attend_on_arrival(slot):
        @pl.when(seq >= slot)
        def _():
            k_arrive(slot)
            attend(slot)

    attend(0)
    pl.semaphore_wait(barrier, greeted)
    pass_down(0)
    for k in range(1, D):
        pl.semaphore_signal(
            met_sem, inc=1, device_id={"dp": lax.rem(dp + k, D)}, device_id_type=MESH
        )

    ready("n")
    xa_buf[0] = dot_general(down[...], nv[...], NT).astype(BF16)

    def xa_copy(k):
        return remote(
            xa_buf.at[0], xa_buf.at[k], xa_send.at[k], xa_recv.at[k], {"tensor": lax.rem(ten + k, T)}
        )

    send([xa_copy(k) for k in range(1, T)], "xa")

    ready("w")

    def dequantised(first, n, put):
        def one(i, carry):
            row = pl.multiple_of(first + i * GROUP, GROUP)
            block = codes[pl.ds(row, GROUP), :].astype(F32)
            put(i, (block * scales[pl.ds(lax.div(row, GROUP), 1), :]).astype(BF16))
            return carry
        lax.fori_loop(0, n // GROUP, one, 0)

    def w_copy(k):
        return remote(
            wst.at[k], wfull.at[k, core], w_send.at[k], w_recv.at[k], {"tensor": lax.rem(ten + k, T)}
        )

    def wc_copy(k, h):
        return remote(wfull.at[k, h], wfull.at[k, h], wc_send.at[k], wc_recv.at[k], {"dp": sibling})

    def send_weights(k):
        def put(i, value):
            wst[k, pl.ds(pl.multiple_of(i * GROUP, GROUP), GROUP), :] = value
        dequantised(lax.rem(ten + k, T) * feats + core * hf, hf, put)
        send([w_copy(k)])

    def own_weights():
        for h in range(2):
            def put(i, value, h=h):
                wfull[0, h, pl.ds(pl.multiple_of(i * GROUP, GROUP), GROUP), :] = value
            dequantised(ten * feats + h * hf, hf, put)


    for n, a in enumerate(tree.relays):
        @pl.when(runs(a))
        def _(a=a):
            k_arrive(a)
            pass_down(a)
        if n + 1 < T:
            send_weights(n + 1)
        for b in tree.after[a]:
            if b in tree.relays:
                @pl.when(seq >= b)
                def _(b=b):
                    attend(b)
            else:
                attend_on_arrival(b)
    for k in range(len(tree.relays) + 1, T):
        send_weights(k)
    coming["w"] = [w_copy(k) for k in range(1, T)]
    for b in tree.final:
        attend_on_arrival(b)

    l_ref[...] = 1.0 / l_ref[...]
    ready("g")

    def partial(slot):
        for g in range(KV):
            total = None
            for i in range(per_kv):
                hp = g * per_kv + i
                factor = jnp.exp2(ms_ref[slot, hp] - m_ref[hp]) * l_ref[hp]
                p = (w_ref[slot, hp].astype(F32) * factor).astype(BF16)
                one = dot(p, gv[hp])
                total = one if total is None else total + one
            acc_ref[g] = total

    def s_copy(a, b, where):
        return remote(rs_out.at[b], rs_in.at[b], s_send.at[b], s_recv.at[b], {"seq": where})

    def up_to(a, b):
        return s_copy(a, b, lax.rem(seq + a - b + S, S))

    def gather(a, keep):
        if a == 0:
            partial(0)
        else:
            @pl.when(seq >= a)
            def _():
                partial(a)

            @pl.when(seq < a)
            def _():
                acc_ref[...] = jnp.zeros(acc_ref.shape, F32)
        for b in tree.children[a]:
            @pl.when(lax.rem(seq - a + S, S) + tree.least[b] <= last)
            def _(b=b):
                s_copy(a, b, seq).wait_recv()
                acc_ref[...] += rs_in[b].astype(F32)
        if keep:
            rs_out[a] = acc_ref[...].astype(BF16)

    for b in tree.up:
        @pl.when(runs(b))
        def _(b=b):
            gather(b, True)
            up_to(tree.parent[b], b).start()

    arrive("xa")
    xat = xa_buf[0].astype(F32)
    for k in range(1, T):
        xat = xat + xa_buf[k].astype(F32)
    xat = xat.astype(BF16)
    arrive("w")
    send([wc_copy(k, core) for k in range(1, T)])
    coming["wc"] = [wc_copy(k, 1 - core) for k in range(1, T)]
    ready("up")
    gather(0, False)
    for g in range(KV):
        dv_buf[0, :, g * HEAD : (g + 1) * HEAD] = acc_ref[g].astype(BF16)

    dv = dv_buf[0]
    gx_buf[0] = dot_general(up[...], dv, NT).astype(BF16)

    def gx_copy(k):
        return remote(
            gx_buf.at[0], gx_buf.at[k], gx_send.at[k], gx_recv.at[k], {"tensor": lax.rem(ten + k, T)}
        )

    def dv_copy(k):
        return remote(
            dv_buf.at[0], dv_buf.at[k], dv_send.at[k], dv_recv.at[k], {"tensor": lax.rem(ten + k, T)}
        )

    send([gx_copy(k) for k in range(1, T)], "gx")
    send([dv_copy(k) for k in range(1, T)], "dv")
    members = D * QUAD
    quads = S // QUAD
    place = lax.rem(seq, QUAD)
    quad = lax.div(seq, QUAD)
    mine = dp * QUAD + place
    wide_a = feats // 128
    wide_b = cols // 128
    n_tiles = (rank // 16) * (wide_a + wide_b)

    def tile_a(i, j):
        n = i * wide_a + j
        return n % members, n // members

    def tile_b(i, j):
        n = (rank // 16) * wide_a + i * wide_b + j
        return n % members, n // members

    per = a_src.shape[1]
    full = n_tiles // members

    def has(piece, slot):
        return slot * members + piece < n_tiles

    part_b = dot(xat, dv)
    for i in range(rank // 16):
        for j in range(cols // 128):
            p, q = tile_b(i, j)
            a_src[p, q] = part_b[i * 16 : i * 16 + 16, j * 128 : j * 128 + 128].astype(BF16)
    arrive("gx")
    gpt = gx_buf[0].astype(F32)
    for k in range(1, T):
        gpt = gpt + gx_buf[k].astype(F32)
    gpt = gpt.astype(BF16)
    for j in range(feats // 128):
        part_a = dot(gpt, nv[:, j * 128 : j * 128 + 128])
        for i in range(rank // 16):
            p, q = tile_a(i, j)
            a_src[p, q] = part_a[i * 16 : i * 16 + 16].astype(BF16)

    def member(k):
        there = lax.rem(dp + lax.div(k, QUAD), D)
        at = lax.rem(place + lax.rem(k, QUAD), QUAD)
        return there * QUAD + at, {"dp": there, "seq": quad * QUAD + at}

    def a_copy(k, slot):
        piece, where = member(k)
        return remote(
            a_src.at[piece, slot], a_rcv.at[k, slot], a_send.at[k, slot], a_recv.at[k, slot], where
        )

    def each(act):
        def one(k, carry):
            act(k)
            return carry
        lax.fori_loop(1, members, one, 0)

    far_first = [
        d * QUAD + z
        for d in sorted(range(D), key=lambda d: -min(d, D - d))
        for z in reversed(range(QUAD))
        if d + z
    ]
    pl.semaphore_wait(met_sem, D - 1)
    for k in far_first:
        for slot in range(full):
            a_copy(k, slot).start()
    for slot in range(full, per):
        @each
        def _(k, slot=slot):
            @pl.when(has(member(k)[0], slot))
            def _():
                a_copy(k, slot).start()
    own_weights()

    def summed(slot):
        def add(k, total):
            a_copy(k, slot).wait_recv()
            return total + a_rcv[k, slot].astype(F32)
        total = lax.fori_loop(1, members, add, a_src[mine, slot].astype(F32))
        b_buf[quad, slot] = total.astype(BF16)

    for slot in range(per):
        if slot < full:
            summed(slot)
        else:
            b_buf[quad, slot] = jnp.zeros((16, 128), BF16)

            @pl.when(has(mine, slot))
            def _(slot=slot):
                summed(slot)

    def b_copy(j):
        there = lax.rem(quad + j, quads)
        return remote(
            b_buf.at[quad], b_buf.at[quad], b_send.at[j], b_recv.at[quad],
            {"seq": there * QUAD + place},
        )

    def b_from(j):
        there = lax.rem(quad + j, quads)
        return remote(
            b_buf.at[there], b_buf.at[there], b_send.at[j], b_recv.at[there],
            {"seq": there * QUAD + place},
        )

    send([b_copy(j) for j in range(1, quads)])
    for j in range(1, quads):
        b_from(j).wait_recv()
    total = b_buf[0].astype(F32)
    for j in range(1, quads):
        total = total + b_buf[j].astype(F32)
    c_buf[...] = total.astype(BF16)

    def d_copy(k, slot):
        where = member(k)[1]
        return remote(
            c_buf.at[slot], d_buf.at[mine, slot], d_send.at[k, slot], d_recv.at[mine, slot], where
        )

    def d_from(k, slot):
        piece, where = member(k)
        return remote(
            c_buf.at[slot], d_buf.at[piece, slot], d_send.at[k, slot], d_recv.at[piece, slot], where
        )

    for k in far_first:
        for slot in range(full):
            d_copy(k, slot).start()
    for slot in range(full, per):
        @pl.when(has(mine, slot))
        def _(slot=slot):
            each(lambda k: d_copy(k, slot).start())
    d_buf[mine] = c_buf[...]

    gp = gpt.T
    arrive("dv")
    arrive("wc")
    width = min(256, hf)
    for n in range(feats // width):
        h, row = n * width // hf, n * width % hf
        at = slice(n * width, (n + 1) * width)
        total = 2.0 * dot(gp, down[:, at])
        for k in range(T):
            total = total + dot_general(dv_buf[k], wfull[k, h, row : row + width, :], NT)
        dn_ref[:, at] = total.astype(BF16)

    for slot in range(per):
        @each
        def _(k, slot=slot):
            @pl.when(has(member(k)[0], slot))
            def _():
                d_from(k, slot).wait_recv()
    factor = 2.0 / math.sqrt(D * S * B)
    for i in range(rank // 16):
        at = slice(i * 16, i * 16 + 16)
        for j in range(wide_a):
            ga_ref[at, j * 128 : j * 128 + 128] = d_buf[tile_a(i, j)].astype(F32) * factor
        for j in range(wide_b):
            gb_ref[at, j * 128 : j * 128 + 128] = d_buf[tile_b(i, j)].astype(F32) * factor

    for c in sent:
        c.wait_send()
    for b, a in tree.parent.items():

        @pl.when(lax.rem(seq - a + S, S) + tree.least[b] <= last)
        def _(a=a, b=b):
            k_copy(a, b, seq).wait_send()

        @pl.when(runs(b))
        def _(b=b):
            up_to(a, b).wait_send()
    for slot in range(per):
        @each
        def _(k, slot=slot):
            @pl.when(has(member(k)[0], slot))
            def _():
                a_copy(k, slot).wait_send()

            @pl.when(has(mine, slot))
            def _():
                d_copy(k, slot).wait_send()


def body(
    shape, queries, keys, output_gradient, normed, document_length, codes, scales,
    adapter_down, adapter_up,
):
    D, S, T = shape
    B = queries.shape[1]
    heads = queries.shape[2] // HEAD
    pairs = heads // 2
    feats = normed.shape[2]
    rank, cols = adapter_up.shape
    members = D * QUAD
    per = -(-(rank // 16) * ((feats + cols) // 128) // members)
    hbm = pl.BlockSpec(memory_space=pltpu.HBM)
    vmem = pl.BlockSpec(memory_space=pltpu.VMEM)
    dma = pltpu.SemaphoreType.DMA
    d_normed, grad_a, grad_b = pl.pallas_call(
        functools.partial(kernel, shape),
        out_shape=(
            jax.ShapeDtypeStruct((B, feats), BF16),
            jax.ShapeDtypeStruct((rank, feats), F32),
            jax.ShapeDtypeStruct((rank, cols), F32),
        ),
        in_specs=[hbm] * 9,
        out_specs=(vmem, vmem, vmem),
        scratch_shapes=[
            pltpu.SMEM(document_length.shape, jnp.int32),
            pltpu.VMEM((S, KV, B, HEAD), BF16),
            pltpu.VMEM((B, heads * HEAD), BF16),
            pltpu.VMEM((pairs, HEAD, 2 * B), BF16),
            pltpu.VMEM((pairs, 2 * B, HEAD), BF16),
            pltpu.VMEM((B, feats), BF16),
            pltpu.VMEM(codes.shape, BF16),
            pltpu.VMEM(scales.shape, F32),
            pltpu.VMEM((rank, feats), BF16),
            pltpu.VMEM((rank, cols), BF16),
            pltpu.VMEM((T, feats // 2, cols), BF16),
            pltpu.VMEM((T, 2, feats // 2, cols), BF16),
            pltpu.VMEM((B, 2 * B), F32),
            pltpu.VMEM((pairs, 1, 2 * B), F32),
            pltpu.VMEM((pairs, 1, 2 * B), F32),
            pltpu.VMEM((S, pairs, 1, 2 * B), F32),
            pltpu.VMEM((S, pairs, B, 2 * B), BF16),
            pltpu.VMEM((KV, B, HEAD), F32),
            pltpu.VMEM((S, KV, B, HEAD), BF16),
            pltpu.VMEM((S, KV, B, HEAD), BF16),
            pltpu.VMEM((T, rank, B), BF16),
            pltpu.VMEM((T, rank, B), BF16),
            pltpu.VMEM((T, B, cols), BF16),
            pltpu.VMEM((members, per, 16, 128), BF16),
            pltpu.VMEM((members, per, 16, 128), BF16),
            pltpu.VMEM((S // QUAD, per, 16, 128), BF16),
            pltpu.VMEM((per, 16, 128), BF16),
            pltpu.VMEM((members, per, 16, 128), BF16),
            pltpu.SemaphoreType.REGULAR,
            dma((9 + heads,)),
            dma((S,)),
            dma((S,)),
            dma((S,)),
            dma((S,)),
            dma((T,)),
            dma((T,)),
            dma((T,)),
            dma((T,)),
            dma((T,)),
            dma((T,)),
            dma((T,)),
            dma((T,)),
            dma((T,)),
            dma((T,)),
            dma((members, per)),
            dma((members, per)),
            dma((S // QUAD,)),
            dma((S // QUAD,)),
            dma((members, per)),
            dma((members, per)),
        ],
        compiler_params=pltpu.CompilerParams(
            collective_id=0, has_side_effects=True, vmem_limit_bytes=40 * 1024 * 1024
        ),
        name="value_backward",
    )(
        *(
            pltpu.with_memory_space_constraint(x, pltpu.HBM)
            for x in (
                queries[0], keys[0], output_gradient[0], normed[0], document_length, codes,
                scales, adapter_down.T, adapter_up,
            )
        )
    )
    return d_normed[None], grad_a.T, grad_b


def solution(mesh):
    shape = tuple(mesh.shape[a] for a in ("dp", "seq", "tensor"))
    split = P("dp", "seq", "tensor")
    placed = (
        split, split, split, split,
        P("dp", None), P(None, "tensor"), P(None, "tensor"), P("tensor", None), P(None, "tensor"),
    )
    return jax.shard_map(
        functools.partial(body, shape),
        mesh=mesh,
        in_specs=placed,
        out_specs=(split, P("tensor", None), P(None, "tensor")),
        check_vma=False,
    )
```
